32 devices in a mesh: rep: 4 (over z), dp: 4 (over y, core), tensor: 2 (over x).
Axes of the slice: x: 2, y: 2, z: 4, core: 2. Of those that a mesh axis runs over, the one named last changes fastest.
Arguments:
- grad_proj: float32 [16, 3072, 1536], P(('rep', 'dp'), 'tensor'), as said below
- grad_conv: float32 [16, 4, 3328], P(('rep', 'dp'), None, 'tensor'), may hold values from -24 to 24
- param_proj: float32 [3072, 1536], P('tensor', 'dp'), may hold values from -6 to 6
- m_proj: float32 [3072, 1536], P('tensor', 'dp'), may hold values from -2 to 2
- v_proj: float32 [3072, 1536], P('tensor', 'dp'), may hold values from 0.02 to 0.2
- ema_proj: float32 [3072, 1536], P(('tensor', 'dp')), may hold values from -6 to 6
- param_conv: float32 [4, 3328], P(None, 'tensor'), may hold values from -3 to 3
- m_conv: float32 [4, 3328], P(None, 'tensor'), may hold values from -2 to 2
- v_conv: float32 [4, 3328], P(None, 'tensor'), may hold values from 0.02 to 0.2
Outputs:
- new_param_proj: float32 [3072, 1536], P('tensor', 'dp')
- new_m_proj: float32 [3072, 1536], P('tensor', 'dp')
- new_v_proj: float32 [3072, 1536], P('tensor', 'dp')
- new_ema_proj: float32 [3072, 1536], P(('tensor', 'dp'))
- weights_proj: bfloat16 [3072, 1536], P('tensor')
- new_param_conv: float32 [4, 3328], P(None, 'tensor')
- new_m_conv: float32 [4, 3328], P(None, 'tensor')
- new_v_conv: float32 [4, 3328], P(None, 'tensor')
The draws below stay inside these ranges and needn't reach their ends.
Inputs may be any that keep to these rules, and one draw needn't show every extreme that they name: `grad_proj`: Real-valued gradients with entries of magnitude below 3100.
All inputs are finite; a program needn't handle non-finite values.
Results may differ from the reference program's by a relative error of at most 0.001.
Values may be sent and summed in bfloat16 or wider, within the bound.
No kernel may reach another device: no remote copies, remote signals or barrier semaphores. Data moves between devices by JAX's collectives and lax.ppermute only.
A program may use at most 128 MiB of HBM per device.

```python
import math
import jax
import jax.numpy as jnp
from jax import lax

D = 1536
INNER = 3072
CONV = 3328
KCONV = 4
REPLICAS = 16


def draw_grad_proj(key, part):
    key_noise, key_rows, key_cols = jax.random.split(key, 3)
    row_trend = jnp.exp(jnp.log(3.0) * jnp.arange(INNER, dtype=jnp.float32) / INNER)
    col_trend = jnp.exp(jnp.log(3.0) * jnp.arange(D, dtype=jnp.float32) / D)
    row_scale = jnp.exp(jax.random.uniform(key_rows, (INNER,), jnp.float32) * jnp.log(10.0)) * row_trend
    col_scale = jnp.exp(jax.random.uniform(key_cols, (D,), jnp.float32) * jnp.log(10.0)) * col_trend
    noise = jnp.clip(jax.random.normal(key_noise, (REPLICAS, INNER, D), jnp.float32), -5.0, 5.0)
    return (0.5 * noise * row_scale[None, :, None] * col_scale[None, None, :]).astype(jnp.float32)


def levels(key, shape, cuts, smallest, top_value):
    level = 1.0
    for dim, shards_of in cuts:
        draws = jax.random.uniform(jax.random.fold_in(jax.random.fold_in(key, 6), dim), (shards_of,), jnp.float32, smallest / len(cuts), top_value / len(cuts))
        level = level * jnp.repeat(jnp.exp(draws), shape[dim] // shards_of).reshape((-1,) + (1,) * (len(shape) - 1 - dim))
    return level


def bell_draw(stream_key, extent, width, limit, pieces=(), held_as=jnp.bfloat16):
    level = levels(stream_key, extent, pieces, -0.22, 0.18) if pieces else 1.0
    drawn = jax.random.normal(stream_key, extent, jnp.float32) * width * level
    return jnp.minimum(jnp.maximum(drawn, -limit), limit).astype(held_as)


def setup_inputs(seed: int = 0) -> dict:
    key_of = jax.random.split(jax.random.key(seed), 10)
    return {
        "grad_proj": draw_grad_proj(jax.random.fold_in(key_of[9], 71), 0),
        "grad_conv": bell_draw(key_of[1], (REPLICAS, KCONV, CONV), 4.0, 24.0, ((0, 16), (2, 2)), jnp.float32),
        "param_proj": bell_draw(key_of[2], (INNER, D), 1.0, 6.0, ((0, 2), (1, 4)), jnp.float32),
        "m_proj": bell_draw(key_of[3], (INNER, D), 0.3, 2.0, ((0, 2), (1, 4)), jnp.float32),
        "v_proj": jnp.clip(jnp.exp(math.log(0.2) - 2.3025851 * jax.random.uniform(key_of[4], (INNER, D), jnp.float32) ** levels(key_of[4], (INNER, D), ((0, 2), (1, 4)), -0.2, 0.2)), 0.02, 0.2),
        "ema_proj": bell_draw(key_of[5], (INNER, D), 1.0, 6.0, ((0, 8),), jnp.float32),
        "param_conv": bell_draw(key_of[6], (KCONV, CONV), 0.5, 3.0, ((1, 2),), jnp.float32),
        "m_conv": bell_draw(key_of[7], (KCONV, CONV), 0.3, 2.0, ((1, 2),), jnp.float32),
        "v_conv": jnp.clip(jnp.exp(math.log(0.2) - 2.3025851 * jax.random.uniform(key_of[8], (KCONV, CONV), jnp.float32) ** levels(key_of[8], (KCONV, CONV), ((1, 2),), -0.2, 0.2)), 0.02, 0.2),
    }


def adamw_step(param_in, first_in, second_in, grad_in):
    first_out = 0.9 * first_in + 0.1 * grad_in
    second_out = 0.95 * second_in + 0.05 * grad_in * grad_in
    bias_one = 1.0 - 0.9 ** 10
    bias_two = 1.0 - 0.95 ** 10
    update = first_out / bias_one / (jnp.sqrt(second_out / bias_two) + 1e-08)
    param_out = param_in - 0.25 * (update + 0.1 * param_in)
    return (param_out, first_out, second_out)

def reference(grad_proj, grad_conv, param_proj, m_proj, v_proj, ema_proj, param_conv, m_conv, v_conv):
    replica_count = grad_proj.shape[0]
    avg_proj = lax.optimization_barrier(jnp.sum(grad_proj, axis=0)) / replica_count
    avg_conv = lax.optimization_barrier(jnp.sum(grad_conv, axis=0)) / replica_count
    grad_norm = jnp.sqrt(jnp.sum(avg_proj * avg_proj) + jnp.sum(avg_conv * avg_conv))
    clip_limit = 0.5 * math.sqrt(INNER * D + KCONV * CONV)
    clip_factor = jnp.minimum(1.0, clip_limit / (grad_norm + 1e-06))
    new_param_proj, new_m_proj, new_v_proj = adamw_step(param_proj, m_proj, v_proj, clip_factor * avg_proj)
    new_param_conv, new_m_conv, new_v_conv = adamw_step(param_conv, m_conv, v_conv, clip_factor * avg_conv)
    weights_proj = new_param_proj.astype(jnp.bfloat16)
    new_ema_proj = 0.9 * ema_proj + 0.1 * new_param_proj
    return (new_param_proj, new_m_proj, new_v_proj, new_ema_proj, weights_proj, new_param_conv, new_m_conv, new_v_conv)
```

```python
import math

import jax
import jax.numpy as jnp
from jax import lax
from jax.sharding import PartitionSpec as P

D = 1536
INNER = 3072
CONV = 3328
KCONV = 4

CORES = 2
REDUCE_CHUNKS = 4
GATHER_CHUNKS = 4
F16_SAFE_REPLICAS = 16


def adamw_step(param_in, first_in, second_in, grad_in):
    first_out = 0.9 * first_in + 0.1 * grad_in
    second_out = 0.95 * second_in + 0.05 * grad_in * grad_in
    bias_one = 1.0 - 0.9**10
    bias_two = 1.0 - 0.95**10
    update = first_out / bias_one / (jnp.sqrt(second_out / bias_two) + 1e-08)
    param_out = param_in - 0.25 * (update + 0.1 * param_in)
    return (param_out, first_out, second_out)


def clip_from(square_sum):
    clip_limit = 0.5 * math.sqrt(INNER * D + KCONV * CONV)
    return jnp.minimum(1.0, clip_limit / (jnp.sqrt(square_sum) + 1e-06))


def butterfly_sum(value, axis):
    size = lax.axis_size(axis)
    step = 1
    while step < size:
        value = value + lax.ppermute(value, axis, [(i, i ^ step) for i in range(size)])
        step *= 2
    return value


def widen(x):
    return x.astype(jnp.float32)


def narrow(x):
    return x.astype(jnp.float16)


def tile_squares(x):
    return jnp.sum(x * x, axis=0, keepdims=True)


def body(grad_proj, grad_conv, param_proj, m_proj, v_proj, ema_proj, param_conv, m_conv, v_conv):
    reps, owners, tensors = lax.axis_size("rep"), lax.axis_size("dp"), lax.axis_size("tensor")
    replica_count = reps * owners
    chips = owners // CORES
    rows, cols = param_proj.shape
    me = lax.axis_index("dp")
    chip, core = me // CORES, me % CORES
    rep = lax.axis_index("rep")

    def core_swap(x):
        return lax.ppermute(x, "dp", [(i, i ^ 1) for i in range(owners)])

    def chip_shift(x, off):
        pairs = [
            (a * CORES + c, ((a + off) % chips) * CORES + c) for a in range(chips) for c in range(CORES)
        ]
        return lax.ppermute(x, "dp", pairs)

    grad = grad_proj[0]
    scale = 1.0 / max(1, 2 ** math.ceil(math.log2(replica_count / F16_SAFE_REPLICAS)))

    conv_avg = butterfly_sum(butterfly_sum(grad_conv[0], "dp"), "rep") / replica_count
    conv_square = jnp.sum(conv_avg * conv_avg)

    parts = REDUCE_CHUNKS
    part_rows = rows // parts
    group_sums = []
    for i in range(parts):

        def block(owner):
            piece = lax.dynamic_slice(grad, (i * part_rows, owner * cols), (part_rows, cols))
            return piece * scale if scale != 1.0 else piece

        from_chips = []
        for off in range(1, chips):
            other = (chip + off) % chips
            got = core_swap(narrow(block(other * CORES + 1 - core)))
            pair_sum = block(other * CORES + core) + widen(got)
            from_chips.append(chip_shift(narrow(pair_sum), off))
        got = core_swap(narrow(block(chip * CORES + 1 - core)))
        total = block(me) + widen(got)
        for got in from_chips:
            total = total + widen(got)
        group_sums.append(total)

    if reps == 4:
        is_end = (rep == 0) | (rep == 3)
        middle_totals, totals = [], []
        for step in range(parts + 2):
            if step < parts:
                payload = narrow(group_sums[step])
                if step >= 2:
                    payload = jnp.where(is_end, payload, middle_totals[step - 2])
            else:
                payload = middle_totals[step - 2]
            got = lax.ppermute(payload, "rep", [(0, 1), (1, 0), (2, 3), (3, 2)])
            if step < parts:
                half = narrow(group_sums[step] + widen(got))
                other_half = lax.ppermute(half, "rep", [(1, 2), (2, 1)])
                middle_totals.append(narrow(widen(half) + widen(other_half)))
            if step >= 2:
                totals.append(jnp.where(is_end, got, middle_totals[step - 2]))
    else:
        totals = [lax.psum(s, "rep") for s in group_sums]

    inverse = 1.0 / (replica_count * scale)
    avgs = [widen(t) * inverse for t in totals]
    square = sum(tile_squares(a) for a in avgs)
    square = square + jnp.where(me == 0, conv_square, 0.0) * (lax.broadcasted_iota(jnp.int32, square.shape, 1) == 0)
    square = butterfly_sum(butterfly_sum(square, "dp"), "tensor")
    clip_factor = clip_from(jnp.sum(square))
    proj_avg = jnp.concatenate(avgs, axis=0)

    weights = adamw_step(param_proj, m_proj, v_proj, clip_factor * proj_avg)[0].astype(jnp.bfloat16)
    weights, proj_avg, clip_factor = lax.optimization_barrier((weights, proj_avg, clip_factor))

    full = jnp.zeros((rows, cols * owners), jnp.bfloat16)
    full = lax.dynamic_update_slice(full, weights, (0, me * cols))
    full = lax.dynamic_update_slice(full, core_swap(weights), (0, (me ^ 1) * cols))
    parts = GATHER_CHUNKS
    part_rows = rows // parts
    for i in range(parts):
        for off in range(1, chips):
            to_chip, from_chip = (chip + off) % chips, (chip - off) % chips
            out_row = ((to_chip * parts) // chips + i) % parts * part_rows
            in_row = ((chip * parts) // chips + i) % parts * part_rows
            piece = lax.dynamic_slice(weights, (out_row, 0), (part_rows, cols))
            got = chip_shift(piece, off)
            got_other = core_swap(got)
            full = lax.dynamic_update_slice(full, got, (in_row, (from_chip * CORES + core) * cols))
            full = lax.dynamic_update_slice(full, got_other, (in_row, (from_chip * CORES + 1 - core) * cols))

    new_param_proj, new_m_proj, new_v_proj = adamw_step(param_proj, m_proj, v_proj, clip_factor * proj_avg)
    new_param_conv, new_m_conv, new_v_conv = adamw_step(param_conv, m_conv, v_conv, clip_factor * conv_avg)
    ema_count = ema_proj.shape[0]
    row_block = lax.dynamic_slice_in_dim(full, me * ema_count, ema_count, 0)
    new_ema_proj = 0.9 * ema_proj + 0.1 * widen(row_block)
    return (
        new_param_proj,
        new_m_proj,
        new_v_proj,
        new_ema_proj,
        full,
        new_param_conv,
        new_m_conv,
        new_v_conv,
    )


def solution(mesh):
    in_specs = (
        P(("rep", "dp"), "tensor", None),
        P(("rep", "dp"), None, "tensor"),
        P("tensor", "dp"),
        P("tensor", "dp"),
        P("tensor", "dp"),
        P(("tensor", "dp"), None),
        P(None, "tensor"),
        P(None, "tensor"),
        P(None, "tensor"),
    )
    out_specs = (
        P("tensor", "dp"),
        P("tensor", "dp"),
        P("tensor", "dp"),
        P(("tensor", "dp"), None),
        P("tensor", None),
        P(None, "tensor"),
        P(None, "tensor"),
        P(None, "tensor"),
    )
    return jax.shard_map(body, mesh=mesh, in_specs=in_specs, out_specs=out_specs, check_vma=False)
```

```python
import math

import jax
import jax.numpy as jnp
from jax import lax
from jax.experimental import pallas as pl
from jax.experimental.pallas import tpu as pltpu
from jax.sharding import PartitionSpec as P

D = 1536
INNER = 3072
CONV = 3328
KCONV = 4

CORES = 2
CHUNKS = 3
LANES = 128
F16_SAFE_REPLICAS = 16
PARAMS = pltpu.CompilerParams(vmem_limit_bytes=16 * 2**20)
LARGE = pltpu.CompilerParams(vmem_limit_bytes=57 * 2**20)
SMALL = pl.CostEstimate(flops=1, bytes_accessed=1024, transcendentals=1)


def adamw_step(param_in, first_in, second_in, grad_in):
    first_out = 0.9 * first_in + 0.1 * grad_in
    second_out = 0.95 * second_in + 0.05 * grad_in * grad_in
    bias_one = 1.0 - 0.9**10
    bias_two = 1.0 - 0.95**10
    update = first_out / bias_one / (jnp.sqrt(second_out / bias_two) + 1e-08)
    param_out = param_in - 0.25 * (update + 0.1 * param_in)
    return (param_out, first_out, second_out)


def clip_from(square_sum):
    clip_limit = 0.5 * math.sqrt(INNER * D + KCONV * CONV)
    return jnp.minimum(1.0, clip_limit / (jnp.sqrt(square_sum) + 1e-06))


def exchange(value, axis, step):
    return lax.ppermute(value, axis, [(i, i ^ step) for i in range(lax.axis_size(axis))])


def steps_of(axis, first=1):
    steps = []
    while first < lax.axis_size(axis):
        steps.append((axis, first))
        first *= 2
    return steps


def widen(x):
    return x.astype(jnp.float32)


def narrow(x):
    return x.astype(jnp.float16)


def together(*values):
    return lax.optimization_barrier(values)


def columns_of(grad, owners, cols):
    rows, width = grad.shape
    if cols % LANES or rows % 8:
        return [lax.dynamic_slice(grad, (0, owner * cols), (rows, cols)) for owner in owners]
    steps = 6
    part = rows // steps

    def kernel(owners_ref, grad_ref, *outs):
        for k, out in enumerate(outs):
            out[...] = grad_ref[:, pl.ds(pl.multiple_of(owners_ref[k] * cols, LANES), cols)]

    return pl.pallas_call(
        kernel,
        grid=(steps,),
        in_specs=[pl.BlockSpec(memory_space=pltpu.SMEM), pl.BlockSpec((part, width), lambda i: (i, 0))],
        out_specs=[pl.BlockSpec((part, cols), lambda i: (i, 0))] * len(owners),
        out_shape=[jax.ShapeDtypeStruct((rows, cols), jnp.float32)] * len(owners),
        cost_estimate=SMALL,
        compiler_params=LARGE,
    )(jnp.stack(owners).astype(jnp.int32), grad)


def step_state(avgs, clip, param, first, second):
    rows, cols = param.shape
    chunks = len(avgs)
    part = rows // chunks

    def kernel(clip_ref, p_ref, m_ref, v_ref, *refs):
        p_out, m_out, v_out = refs[-3:]
        for k in range(chunks):

            @pl.when(pl.program_id(0) == k)
            def _():
                p, m, v = adamw_step(p_ref[...], m_ref[...], v_ref[...], clip_ref[0, 0] * refs[k][...])
                p_out[...], m_out[...], v_out[...] = p, m, v

    chunk = pl.BlockSpec((part, cols), lambda i: (i, 0))
    return pl.pallas_call(
        kernel,
        grid=(chunks,),
        in_specs=[pl.BlockSpec(memory_space=pltpu.SMEM)]
        + [chunk] * 3
        + [pl.BlockSpec((part, cols), lambda i: (0, 0))] * chunks,
        out_specs=[chunk] * 3,
        out_shape=[jax.ShapeDtypeStruct((rows, cols), jnp.float32)] * 3,
        cost_estimate=SMALL,
        compiler_params=PARAMS,
    )(clip, param, first, second, *avgs)


def place(full, shape, row_block, chip, core, mine, theirs):
    part, cols = mine.shape
    where = jnp.stack([jnp.int32(x) for x in (row_block, chip, core)])

    def kernel(where_ref, mine_ref, theirs_ref, *refs):
        out_ref = refs[-1]

        @pl.when(where_ref[2] == 0)
        def _():
            out_ref[:, :cols] = mine_ref[...]
            out_ref[:, cols:] = theirs_ref[...]

        @pl.when(where_ref[2] != 0)
        def _():
            out_ref[:, :cols] = theirs_ref[...]
            out_ref[:, cols:] = mine_ref[...]

    block = pl.BlockSpec((part, cols), lambda i, where: (0, 0))
    so_far = [] if full is None else [full]
    return pl.pallas_call(
        kernel,
        grid_spec=pltpu.PrefetchScalarGridSpec(
            num_scalar_prefetch=1,
            grid=(1,),
            in_specs=[block, block] + [pl.BlockSpec(memory_space=pl.ANY)] * len(so_far),
            out_specs=pl.BlockSpec((part, CORES * cols), lambda i, where: (where[0], where[1])),
        ),
        out_shape=jax.ShapeDtypeStruct(shape, jnp.bfloat16),
        input_output_aliases={3: 0} if so_far else {},
        cost_estimate=SMALL,
        compiler_params=PARAMS,
    )(where, mine, theirs, *so_far)


def average(so_far, ema, chip, core, mine, theirs):
    rows, width = ema.shape
    cols = mine.shape[1]
    where = jnp.stack([chip, core]).astype(jnp.int32)

    def kernel(where_ref, ema_ref, mine_ref, theirs_ref, *refs):
        out_ref = refs[-1]
        for c in range(CORES):

            @pl.when(where_ref[1] == c)
            def _():
                for k, ref in enumerate((mine_ref, theirs_ref) if c == 0 else (theirs_ref, mine_ref)):
                    at = slice(k * cols, (k + 1) * cols)
                    out_ref[:, at] = 0.9 * ema_ref[:, at] + 0.1 * widen(ref[...])

    so_far = [] if so_far is None else [so_far]
    block = pl.BlockSpec((rows, CORES * cols), lambda i, where: (0, where[0]))
    piece = pl.BlockSpec((rows, cols), lambda i, where: (0, 0))
    return pl.pallas_call(
        kernel,
        grid_spec=pltpu.PrefetchScalarGridSpec(
            num_scalar_prefetch=1,
            grid=(1,),
            in_specs=[block, piece, piece] + [pl.BlockSpec(memory_space=pl.ANY)] * len(so_far),
            out_specs=block,
        ),
        out_shape=jax.ShapeDtypeStruct(ema.shape, jnp.float32),
        input_output_aliases={4: 0} if so_far else {},
        cost_estimate=SMALL,
        compiler_params=PARAMS,
    )(where, ema, mine, theirs, *so_far)


def body(grad_proj, grad_conv, param_proj, m_proj, v_proj, ema_proj, param_conv, m_conv, v_conv):
    reps, owners = lax.axis_size("rep"), lax.axis_size("dp")
    replica_count = reps * owners
    chips = owners // CORES
    rows, cols = param_proj.shape
    shape = (rows, cols * owners)
    me = lax.axis_index("dp")
    chip, core = me // CORES, me % CORES
    rep = lax.axis_index("rep")
    part_rows = rows // CHUNKS
    aligned = cols % LANES == 0 and part_rows % 16 == 0

    def core_swap(x):
        return exchange(x, "dp", 1)

    def chip_shift(x, off):
        pairs = [
            (a * CORES + c, ((a + off) % chips) * CORES + c) for a in range(chips) for c in range(CORES)
        ]
        return lax.ppermute(x, "dp", pairs)

    def chunk(x, i):
        return x[i * part_rows : (i + 1) * part_rows]

    scale = 1.0 / max(1, 2 ** math.ceil(math.log2(replica_count / F16_SAFE_REPLICAS)))
    inverse = 1.0 / (replica_count * scale)
    grad = grad_proj[0]

    def scaled(x):
        return x * scale if scale != 1.0 else x

    others = [(chip + off) % chips for off in range(1, chips)]
    owners_needed = [other * CORES + 1 - core for other in (*others, chip)]
    owners_needed += [other * CORES + core for other in (*others, chip)]
    blocks = columns_of(grad, owners_needed, cols)
    to_swap, to_keep = blocks[:chips], blocks[chips:]
    conv_steps = [*steps_of("rep"), ("dp", 1), *steps_of("dp", CORES)]
    conv_sum = grad_conv[0]

    def conv_hop(first=None):
        sent = conv_sum if first is None else together(conv_sum, first)[0]
        return sent, exchange(sent, *conv_steps.pop(0))

    spans = [(0, part_rows), (part_rows, rows)]
    to_send = [[] for _ in others]
    last = None
    for start, stop in spans:
        swapped = [core_swap(x[start:stop]) for x in to_swap[:-1]]
        own_conv, got_conv = conv_hop(last)
        *swapped, own_conv, got_conv = together(*swapped, own_conv, got_conv)
        conv_sum = own_conv + got_conv
        for n, got in enumerate(swapped):
            last = narrow(scaled(to_keep[n][start:stop] + got))
            to_send[n].append(last)
    own_conv, got_conv = conv_hop(last)
    own_keep, got = together(to_keep[-1], core_swap(to_swap[-1]))
    own_sum = scaled(own_keep + got)

    def outgoing(n, i):
        return to_send[n][0] if i == 0 else to_send[n][1][(i - 1) * part_rows : i * part_rows]

    avgs, squares = [None] * CHUNKS, [None] * CHUNKS
    sums, halves, totals = {}, {}, {}
    is_end = (rep == 0) | (rep == 3)
    moving = {}

    def set_average(i, total):
        avgs[i] = total * inverse
        squares[i] = jnp.sum(avgs[i] * avgs[i], axis=0, keepdims=True)

    for r in range(CHUNKS + 3 if reps == 4 else CHUNKS + 1):
        if r == 1:
            moving["own_conv"], moving["conv"] = own_conv, got_conv
        names = list(moving)
        there = dict(zip(names, together(*[moving[k] for k in names]))) if names else {}
        moving = {}
        own = chunk(own_sum, r - 1) if 0 <= r - 1 < CHUNKS else None
        if own is not None:
            for n in range(len(others)):
                own = own + widen(there["chips", n])
            sums[r - 1] = narrow(own) if reps == 4 else own
        if "pair" in there:
            i = r - 2
            if i < CHUNKS:
                halves[i] = narrow(widen(sums[i]) + widen(there["pair"]))
            if i >= 2:
                set_average(i - 2, widen(jnp.where(is_end, there["pair"], totals[i - 2])))
                if i - 2 < CHUNKS - 1:
                    moving["square"] = squares[i - 2]
        if "middle" in there:
            i = r - 3
            totals[i] = narrow(widen(halves[i]) + widen(there["middle"]))
        if "conv" in there:
            conv_sum = there["own_conv"] + there["conv"]
        if "square" in there:
            squares[r - 5] = there["square"]

        if r < CHUNKS:
            for n in range(len(others)):
                payload = outgoing(n, r)
                if there:
                    payload = together(payload, next(iter(there.values())))[0]
                moving["chips", n] = chip_shift(payload, n + 1)
        if reps == 4:
            i = r - 1
            if 0 <= i < CHUNKS + 2:
                if i < 2:
                    payload = sums[i]
                elif i < CHUNKS:
                    payload = jnp.where(is_end, sums[i], totals[i - 2])
                else:
                    payload = totals[i - 2]
                moving["pair"] = lax.ppermute(payload, "rep", [(0, 1), (1, 0), (2, 3), (3, 2)])
            if 0 <= r - 2 < CHUNKS:
                moving["middle"] = lax.ppermute(halves[r - 2], "rep", [(1, 2), (2, 1)])
        if conv_steps and r >= 2:
            moving["own_conv"], moving["conv"] = conv_hop()
    if reps == 4:
        for name in ("pair",):
            got = moving[name]
        set_average(CHUNKS - 1, widen(jnp.where(is_end, got, totals[CHUNKS - 1])))
    else:
        for i in range(CHUNKS):
            set_average(i, lax.psum(sums[i], "rep"))
    while conv_steps:
        conv_sum = sum(conv_hop())
    conv_avg = conv_sum / replica_count
    conv_square = jnp.sum(conv_avg * conv_avg)

    square = sum(squares[1:], squares[0])
    square = square + jnp.where(me == 0, conv_square, 0.0) * (lax.broadcasted_iota(jnp.int32, square.shape, 1) == 0)
    for step in [*steps_of("dp"), *steps_of("tensor")]:
        square = square + exchange(square, *step)
    clip_factor = clip_from(jnp.sum(square, keepdims=True))

    def new_weights(i):
        return adamw_step(chunk(param_proj, i), chunk(m_proj, i), chunk(v_proj, i), clip_factor * avgs[i])[0]

    if not (aligned and chips == 2 and reps % 2 == 0 and CHUNKS == 3):
        weights = [new_weights(i).astype(jnp.bfloat16) for i in range(CHUNKS)]
        weights = jnp.concatenate(weights, axis=0)
        full = jnp.zeros(shape, jnp.bfloat16)
        for piece, owner in ((weights, me), (core_swap(weights), me ^ 1)):
            full = lax.dynamic_update_slice(full, piece, (0, owner * cols))
        for off in range(1, chips):
            got = chip_shift(weights, off)
            from_chip = (chip - off) % chips
            for piece, owner in ((got, from_chip * CORES + core), (core_swap(got), from_chip * CORES + 1 - core)):
                full = lax.dynamic_update_slice(full, piece, (0, owner * cols))
        results = adamw_step(param_proj, m_proj, v_proj, clip_factor * jnp.concatenate(avgs))
        conv_results = adamw_step(param_conv, m_conv, v_conv, clip_factor * conv_avg)
        ema_count = ema_proj.shape[0]
        row_block = lax.dynamic_slice_in_dim(full, me * ema_count, ema_count, 0)
        return (*results, 0.9 * ema_proj + 0.1 * widen(row_block), full, *conv_results)

    odd = rep % 2 == 1

    def either(values):
        return jnp.where(odd, values[1], values[0])

    inputs = [[chunk(x, i) for i in range(CHUNKS)] for x in (param_proj, m_proj, v_proj)] + [avgs]
    p, m, v, g = (either(values) for values in inputs)
    first = adamw_step(p, m, v, clip_factor * g)[0].astype(jnp.bfloat16)
    got_first = chip_shift(first, 1)
    clip, _ = together(clip_factor, first)
    p, m, v, g = (values[2] for values in inputs)
    third = adamw_step(p, m, v, clip * g)[0].astype(jnp.bfloat16)
    clip, _ = together(clip, third)
    results = step_state(avgs, clip, param_proj, m_proj, v_proj)
    weights = results[0].astype(jnp.bfloat16)
    weights, got_first, third = together(weights, got_first, third)

    got_third = chip_shift(third, 1)
    got_second = exchange(got_first, "rep", 1)
    got_first_other = core_swap(got_first)
    partner = core_swap(weights)
    full = None
    for i in range(CHUNKS):
        full = place(full, shape, i, chip, core, chunk(weights, i), chunk(partner, i))
    ema_rows = ema_proj.shape[0]

    def for_average(x):
        return lax.dynamic_slice_in_dim(x, me * ema_rows, ema_rows, 0)

    new_ema = average(None, ema_proj, chip, core, for_average(weights), for_average(partner))
    clip, _ = together(clip, new_ema)
    conv_results = adamw_step(param_conv, m_conv, v_conv, clip * conv_avg)
    got_first, got_first_other, _ = together(got_first, got_first_other, conv_results[0])
    full = place(full, shape, jnp.where(odd, 1, 0), 1 - chip, core, got_first, got_first_other)
    got_third, got_second, full = together(got_third, got_second, full)
    got_third_other, got_second_other = core_swap(got_third), core_swap(got_second)
    full = place(full, shape, jnp.where(odd, 0, 1), 1 - chip, core, got_second, got_second_other)
    full = place(full, shape, 2, 1 - chip, core, got_third, got_third_other)

    def assembled(a, b, c):
        return for_average(jnp.concatenate([jnp.where(odd, b, a), jnp.where(odd, a, b), c]))

    new_ema = average(
        new_ema,
        ema_proj,
        1 - chip,
        core,
        assembled(got_first, got_second, got_third),
        assembled(got_first_other, got_second_other, got_third_other),
    )
    return (*results, new_ema, full, *conv_results)


def solution(mesh):
    in_specs = (
        P(("rep", "dp"), "tensor", None),
        P(("rep", "dp"), None, "tensor"),
        P("tensor", "dp"),
        P("tensor", "dp"),
        P("tensor", "dp"),
        P(("tensor", "dp"), None),
        P(None, "tensor"),
        P(None, "tensor"),
        P(None, "tensor"),
    )
    out_specs = (
        P("tensor", "dp"),
        P("tensor", "dp"),
        P("tensor", "dp"),
        P(("tensor", "dp"), None),
        P("tensor", None),
        P(None, "tensor"),
        P(None, "tensor"),
        P(None, "tensor"),
    )
    return jax.shard_map(body, mesh=mesh, in_specs=in_specs, out_specs=out_specs, check_vma=False)
```

```python
import math

import jax
import jax.numpy as jnp
from jax import lax
from jax.experimental import pallas as pl
from jax.experimental.pallas import tpu as pltpu
from jax.sharding import PartitionSpec as P

D = 1536
INNER = 3072
CONV = 3328
KCONV = 4

CORES = 2
CHUNKS = 3
LANES = 128
F16_SAFE_REPLICAS = 16
PARAMS = pltpu.CompilerParams(vmem_limit_bytes=16 * 2**20)
SMALL = pl.CostEstimate(flops=1, bytes_accessed=1024, transcendentals=1)


def adamw_step(param_in, first_in, second_in, grad_in):
    first_out = 0.9 * first_in + 0.1 * grad_in
    second_out = 0.95 * second_in + 0.05 * grad_in * grad_in
    bias_one = 1.0 - 0.9**10
    bias_two = 1.0 - 0.95**10
    update = first_out / bias_one / (jnp.sqrt(second_out / bias_two) + 1e-08)
    param_out = param_in - 0.25 * (update + 0.1 * param_in)
    return (param_out, first_out, second_out)


def clip_from(square_sum):
    clip_limit = 0.5 * math.sqrt(INNER * D + KCONV * CONV)
    return jnp.minimum(1.0, clip_limit / (jnp.sqrt(square_sum) + 1e-06))


def exchange(value, axis, step):
    return lax.ppermute(value, axis, [(i, i ^ step) for i in range(lax.axis_size(axis))])


def steps_of(axis, first=1):
    steps = []
    while first < lax.axis_size(axis):
        steps.append((axis, first))
        first *= 2
    return steps


def widen(x):
    return x.astype(jnp.float32)


def narrow(x):
    return x.astype(jnp.float16)


def together(*values):
    return lax.optimization_barrier(values)


def step_state(avgs, clip, param, first, second):
    rows, cols = param.shape
    chunks = len(avgs)
    part = rows // chunks

    def kernel(clip_ref, p_ref, m_ref, v_ref, *refs):
        p_out, m_out, v_out, w_out, last_out = refs[-5:]
        for k in range(chunks):

            @pl.when(pl.program_id(0) == k)
            def _():
                p, m, v = adamw_step(p_ref[...], m_ref[...], v_ref[...], clip_ref[0, 0] * refs[k][...])
                p_out[...], m_out[...], v_out[...] = p, m, v
                w_out[...] = p.astype(jnp.bfloat16)
                last_out[...] = p.astype(jnp.bfloat16)

    chunk = pl.BlockSpec((part, cols), lambda i: (i, 0))
    alone = pl.BlockSpec((part, cols), lambda i: (0, 0))
    whole = jax.ShapeDtypeStruct((rows, cols), jnp.float32)
    return pl.pallas_call(
        kernel,
        grid=(chunks,),
        in_specs=[pl.BlockSpec(memory_space=pltpu.SMEM)] + [chunk] * 3 + [alone] * chunks,
        out_specs=[chunk] * 4 + [alone],
        out_shape=[whole, whole, whole]
        + [jax.ShapeDtypeStruct((rows, cols), jnp.bfloat16), jax.ShapeDtypeStruct((part, cols), jnp.bfloat16)],
        cost_estimate=SMALL,
        compiler_params=PARAMS,
    )(clip, param, first, second, *avgs)


def place(so_far, shape, ema, me, chip, core, pieces):
    rows, width = shape
    columns = width // 2
    cols = columns // CORES
    ema_rows = ema.shape[0]
    where = jnp.stack([jnp.int32(x) for x in (me, chip, core, *(block for block, _, _ in pieces))])
    values = [x for _, mine, theirs in pieces for x in (mine, theirs)]

    def kernel(where_ref, ema_ref, *refs):
        full_out, ema_out, near, ema_near, new_near, sems = refs[-6:]
        here = pl.ds(pl.multiple_of(where_ref[1] * columns, LANES), columns)
        load = pltpu.make_async_copy(ema_ref.at[:, here], ema_near, sems.at[0])
        load.start()
        stores = []
        for k in range(len(pieces)):
            mine, theirs = refs[2 * k], refs[2 * k + 1]
            at = pl.ds(pl.multiple_of(where_ref[3 + k] * mine.shape[0], 16), mine.shape[0])

            @pl.when(where_ref[2] == 0)
            def _():
                near[at, :cols] = mine[...]
                near[at, cols:] = theirs[...]

            @pl.when(where_ref[2] != 0)
            def _():
                near[at, :cols] = theirs[...]
                near[at, cols:] = mine[...]

            stores.append(pltpu.make_async_copy(near.at[at, :], full_out.at[at, here], sems.at[2 + k]))
            stores[-1].start()
        load.wait()
        mine_rows = near[pl.ds(pl.multiple_of(where_ref[0] * ema_rows, 16), ema_rows), :]
        new_near[...] = 0.9 * ema_near[...] + 0.1 * widen(mine_rows)
        stores.append(pltpu.make_async_copy(new_near, ema_out.at[:, here], sems.at[1]))
        stores[-1].start()
        for store in stores:
            store.wait()

    far = pl.BlockSpec(memory_space=pltpu.HBM)
    return pl.pallas_call(
        kernel,
        in_specs=[pl.BlockSpec(memory_space=pltpu.SMEM), far]
        + [pl.BlockSpec(memory_space=pltpu.VMEM)] * len(values)
        + [far] * len(so_far),
        out_specs=[far, far],
        out_shape=[jax.ShapeDtypeStruct(shape, jnp.bfloat16), jax.ShapeDtypeStruct(ema.shape, jnp.float32)],
        input_output_aliases={2 + len(values) + i: i for i in range(len(so_far))},
        scratch_shapes=[
            pltpu.VMEM((rows, columns), jnp.bfloat16),
            pltpu.VMEM((ema_rows, columns), jnp.float32),
            pltpu.VMEM((ema_rows, columns), jnp.float32),
            pltpu.SemaphoreType.DMA((2 + len(pieces),)),
        ],
        cost_estimate=SMALL,
        compiler_params=PARAMS,
    )(where, ema, *values, *so_far)


def body(grad_proj, grad_conv, param_proj, m_proj, v_proj, ema_proj, param_conv, m_conv, v_conv):
    reps, owners = lax.axis_size("rep"), lax.axis_size("dp")
    replica_count = reps * owners
    chips = owners // CORES
    rows, cols = param_proj.shape
    shape = (rows, cols * owners)
    me = lax.axis_index("dp")
    chip, core = me // CORES, me % CORES
    rep = lax.axis_index("rep")
    part_rows = rows // CHUNKS
    aligned = cols % LANES == 0 and part_rows % 16 == 0
    line = reps == 4

    def core_swap(x):
        return exchange(x, "dp", 1)

    def chip_shift(x, off):
        pairs = [
            (a * CORES + c, ((a + off) % chips) * CORES + c) for a in range(chips) for c in range(CORES)
        ]
        return lax.ppermute(x, "dp", pairs)

    def chunk(x, i):
        return x[i * part_rows : (i + 1) * part_rows]

    odd = rep % 2 == 1

    def either(values):
        return jnp.where(odd, values[1], values[0])

    scale = 1.0 / max(1, 2 ** math.ceil(math.log2(replica_count / F16_SAFE_REPLICAS)))
    inverse = 1.0 / (replica_count * scale)
    grad = grad_proj[0]

    def scaled(x):
        return x * scale if scale != 1.0 else x

    def block(owner_chip, owner_core, i):
        start = i * part_rows
        if owners != 4:
            owner = owner_chip * CORES + owner_core
            return scaled(lax.dynamic_slice(grad, (start, owner * cols), (part_rows, cols)))
        a, b, c, d = (grad[start : start + part_rows, n * cols : (n + 1) * cols] for n in range(owners))
        return scaled(jnp.where(owner_chip == 0, jnp.where(owner_core == 0, a, b), jnp.where(owner_core == 0, c, d)))

    targets = [(chip + off) % chips for off in (*range(1, chips), 0)]

    def gift(n, i):
        return core_swap(narrow(block(targets[n], 1 - core, i)))

    def chip_sum(n, i):
        return block(targets[n], core, i) + widen(gifts[n, i])

    gifts = {(n, 0): gift(n, 0) for n in range(chips)}
    gifts.update({(n, i): gift(n, i) for i in range(1, CHUNKS) for n in range(chips)})

    avgs, squares = [None] * CHUNKS, [None] * CHUNKS
    sums, halves, totals = {}, {}, {}
    is_end = (rep == 0) | (rep == 3)
    conv_steps = [*steps_of("rep"), *steps_of("dp")]
    conv_sum = grad_conv[0]
    chosen = [[chunk(x, i) for i in range(CHUNKS)] for x in (param_proj, m_proj, v_proj)]
    chosen = [either(values) for values in chosen]

    def average_of(total):
        return widen(total) * inverse

    def square_of(total):
        value = average_of(total)
        return jnp.sum(value * value, axis=0, keepdims=True)

    moving, outgoing = {}, {}
    rounds = CHUNKS + 2 if line else CHUNKS
    for r in range(rounds + 1):
        names = list(moving)
        there = dict(zip(names, together(*[moving[k] for k in names]))) if names else {}
        moving, waiting = {}, {}
        for k, value in there.items():
            if k[0] == "gift":
                gifts[k[1:]] = value
            elif k[0] == "average":
                avgs[k[1]] = value
            elif k[0] == "square":
                squares[k[1]] = value
            elif k[0] == "chosen":
                chosen[k[1]] = value
            elif k[0] == "outgoing":
                outgoing[k[1:]] = value

        if 0 <= r - 1 < CHUNKS:
            own = there["own", 2] if r == 3 else chip_sum(chips - 1, r - 1)
            for n in range(chips - 1):
                own = own + widen(there["chips", n])
            sums[r - 1] = narrow(own) if line else lax.psum(own, "rep")
        if ("pair", 0) in there:
            i = r - 2
            if i < CHUNKS:
                halves[i] = narrow(widen(sums[i]) + widen(there["pair", 0]))
            if i >= 2:
                waiting["average", i - 2] = average_of(jnp.where(is_end, there["pair", 0], totals[i - 2]))
        if ("middle", 0) in there:
            totals[r - 3] = narrow(widen(halves[r - 3]) + widen(there["middle", 0]))
            if r < rounds:
                waiting["square", r - 3] = square_of(totals[r - 3])
            else:
                squares[r - 3] = square_of(totals[r - 3])
        if ("conv", 0) in there:
            conv_sum = there["own conv", 0] + there["conv", 0]

        payloads = []
        if r < CHUNKS:
            for n in range(chips - 1):
                payloads.append(outgoing[n, r] if r else narrow(chip_sum(n, r)))
                moving["chips", n] = chip_shift(payloads[-1], n + 1)
        if r == 0:
            for k, value in gifts.items():
                if k[1] or k[0] == chips - 1:
                    moving["gift", *k] = value
        if line:
            i = r - 1
            if 0 <= i < CHUNKS + 2:
                if i < 2:
                    payload = sums[i]
                elif i < CHUNKS:
                    payload = jnp.where(is_end, sums[i], totals[i - 2])
                else:
                    payload = totals[i - 2]
                payloads.append(payload)
                moving["pair", 0] = lax.ppermute(payload, "rep", [(0, 1), (1, 0), (2, 3), (3, 2)])
            if 0 <= r - 2 < CHUNKS:
                payloads.append(halves[r - 2])
                moving["middle", 0] = lax.ppermute(halves[r - 2], "rep", [(1, 2), (2, 1)])
        if conv_steps and payloads:
            sent, *_ = together(conv_sum, *payloads)
            moving["own conv", 0] = sent
            moving["conv", 0] = exchange(sent, *conv_steps.pop(0))
        if r == 2:
            gifts[chips - 1, r] = together(gifts[chips - 1, r], moving["conv", 0])[0]
            moving["own", r] = chip_sum(chips - 1, r)
        if r + 1 < CHUNKS:
            for n in range(chips - 1):
                ready = moving["conv", 0]
                if r == 0:
                    gifts[n, 1], ready = together(moving.pop(("gift", n, 1)), ready)
                else:
                    gifts[n, r + 1], ready = together(gifts[n, r + 1], ready)
                moving["conv", 0] = ready
                moving["outgoing", n, r + 1] = narrow(chip_sum(n, r + 1))
        if r == rounds - 2:
            for n in range(len(chosen)):
                waiting["chosen", n] = chosen[n]
        moving.update(waiting)

    if not line:
        avgs = [average_of(sums[i]) for i in range(CHUNKS)]
        squares = [square_of(sums[i]) for i in range(CHUNKS)]
    for step in conv_steps:
        conv_sum = conv_sum + exchange(conv_sum, *step)
    conv_avg = conv_sum / replica_count
    conv_square = jnp.sum(conv_avg * conv_avg)

    square = sum(squares[1:], squares[0])
    square = square + jnp.where(me == 0, conv_square, 0.0) * (lax.broadcasted_iota(jnp.int32, square.shape, 1) == 0)
    hops = [*steps_of("dp"), *steps_of("tensor")]
    for step in hops if not line else hops[:-1]:
        square = square + exchange(square, *step)
    if line:
        size, step = lax.axis_size("tensor"), hops[-1][1]
        across = [(a * size + t, (a ^ 1) * size + (t ^ step)) for a in range(reps) for t in range(size)]
        theirs = lax.ppermute(square, ("rep", "tensor"), across)
        inner, other = exchange(square, "rep", 1), exchange(square, *hops[-1])
        square = jnp.where(is_end, inner, square) + jnp.where(is_end, theirs, other)
        arrived = moving["pair", 0]
        for n in range(CHUNKS - 1):
            if avgs[n] is None:
                avgs[n] = moving["average", n]
    clip_factor = clip_from(jnp.sum(square, keepdims=True))

    def last_average(after):
        if not line:
            return avgs[-1]
        return average_of(jnp.where(is_end, together(arrived, after)[0], totals[CHUNKS - 1]))

    if not (aligned and chips == 2 and reps % 2 == 0 and CHUNKS == 3):
        avgs[-1] = last_average(clip_factor)
        results = adamw_step(param_proj, m_proj, v_proj, clip_factor * jnp.concatenate(avgs))
        weights = results[0].astype(jnp.bfloat16)
        full = jnp.zeros(shape, jnp.bfloat16)
        for piece, owner in ((weights, me), (core_swap(weights), me ^ 1)):
            full = lax.dynamic_update_slice(full, piece, (0, owner * cols))
        for off in range(1, chips):
            got = chip_shift(weights, off)
            from_chip = (chip - off) % chips
            for piece, owner in ((got, from_chip * CORES + core), (core_swap(got), from_chip * CORES + 1 - core)):
                full = lax.dynamic_update_slice(full, piece, (0, owner * cols))
        conv_results = adamw_step(param_conv, m_conv, v_conv, clip_factor * conv_avg)
        ema_count = ema_proj.shape[0]
        row_block = lax.dynamic_slice_in_dim(full, me * ema_count, ema_count, 0)
        return (*results, 0.9 * ema_proj + 0.1 * widen(row_block), full, *conv_results)

    g = either(avgs)
    p, m, v = chosen
    first = adamw_step(p, m, v, clip_factor * g)[0].astype(jnp.bfloat16)
    got_first = chip_shift(first, 1)
    avgs[-1] = last_average(first)
    *results, weights, third = step_state(avgs, clip_factor, param_proj, m_proj, v_proj)
    weights, got_first, third = together(weights, got_first, third)

    got_third = chip_shift(third, 1)
    got_second = exchange(got_first, "rep", 1)
    got_first_other = core_swap(got_first)
    so_far = place([], shape, ema_proj, me, chip, core, [(0, weights, core_swap(weights))])
    clip, _ = together(clip_factor, so_far[0])
    conv_results = adamw_step(param_conv, m_conv, v_conv, clip * conv_avg)
    got_third, got_second, *_ = together(got_third, got_second, *so_far, conv_results[0])
    first_block = jnp.where(odd, 1, 0)
    pieces = [
        (first_block, got_first, got_first_other),
        (1 - first_block, got_second, core_swap(got_second)),
        (2, got_third, core_swap(got_third)),
    ]
    full, new_ema = place(so_far, shape, ema_proj, me, 1 - chip, core, pieces)
    return (*results, new_ema, full, *conv_results)


def solution(mesh):
    in_specs = (
        P(("rep", "dp"), "tensor", None),
        P(("rep", "dp"), None, "tensor"),
        P("tensor", "dp"),
        P("tensor", "dp"),
        P("tensor", "dp"),
        P(("tensor", "dp"), None),
        P(None, "tensor"),
        P(None, "tensor"),
        P(None, "tensor"),
    )
    out_specs = (
        P("tensor", "dp"),
        P("tensor", "dp"),
        P("tensor", "dp"),
        P(("tensor", "dp"), None),
        P("tensor", None),
        P(None, "tensor"),
        P(None, "tensor"),
        P(None, "tensor"),
    )
    return jax.shard_map(body, mesh=mesh, in_specs=in_specs, out_specs=out_specs, check_vma=False)
```

```python
import math

import jax
import jax.numpy as jnp
from jax import lax
from jax.experimental import pallas as pl
from jax.experimental.pallas import tpu as pltpu
from jax.sharding import PartitionSpec as P

D = 1536
INNER = 3072
CONV = 3328
KCONV = 4

CORES = 2
CHUNKS = 3
LANES = 128
F16_SAFE_REPLICAS = 16
PARAMS = pltpu.CompilerParams(vmem_limit_bytes=16 * 2**20)
SMALL = pl.CostEstimate(flops=1, bytes_accessed=1024, transcendentals=1)


def adamw_step(param_in, first_in, second_in, grad_in):
    first_out = 0.9 * first_in + 0.1 * grad_in
    second_out = 0.95 * second_in + 0.05 * grad_in * grad_in
    bias_one = 1.0 - 0.9**10
    bias_two = 1.0 - 0.95**10
    update = first_out / bias_one / (jnp.sqrt(second_out / bias_two) + 1e-08)
    param_out = param_in - 0.25 * (update + 0.1 * param_in)
    return (param_out, first_out, second_out)


def clip_from(square_sum):
    clip_limit = 0.5 * math.sqrt(INNER * D + KCONV * CONV)
    return jnp.minimum(1.0, clip_limit / (jnp.sqrt(square_sum) + 1e-06))


def exchange(value, axis, step):
    return lax.ppermute(value, axis, [(i, i ^ step) for i in range(lax.axis_size(axis))])


def steps_of(axis, first=1):
    steps = []
    while first < lax.axis_size(axis):
        steps.append((axis, first))
        first *= 2
    return steps


def widen(x):
    return x.astype(jnp.float32)


def narrow(x):
    return x.astype(jnp.float16)


def together(*values):
    return lax.optimization_barrier(values)


def step_state(avgs, clip, param, first, second):
    rows, cols = param.shape
    chunks = len(avgs)
    part = rows // chunks

    def kernel(clip_ref, p_ref, m_ref, v_ref, *refs):
        p_out, m_out, v_out, w_out, last_out = refs[-5:]
        for k in range(chunks):

            @pl.when(pl.program_id(0) == k)
            def _():
                p, m, v = adamw_step(p_ref[...], m_ref[...], v_ref[...], clip_ref[0, 0] * refs[k][...])
                p_out[...], m_out[...], v_out[...] = p, m, v
                w_out[...] = p.astype(jnp.bfloat16)
                last_out[...] = p.astype(jnp.bfloat16)

    chunk = pl.BlockSpec((part, cols), lambda i: (i, 0))
    alone = pl.BlockSpec((part, cols), lambda i: (0, 0))
    whole = jax.ShapeDtypeStruct((rows, cols), jnp.float32)
    return pl.pallas_call(
        kernel,
        grid=(chunks,),
        in_specs=[pl.BlockSpec(memory_space=pltpu.SMEM)] + [chunk] * 3 + [alone] * chunks,
        out_specs=[chunk] * 4 + [alone],
        out_shape=[whole, whole, whole]
        + [jax.ShapeDtypeStruct((rows, cols), jnp.bfloat16), jax.ShapeDtypeStruct((part, cols), jnp.bfloat16)],
        cost_estimate=SMALL,
        compiler_params=PARAMS,
    )(clip, param, first, second, *avgs)


def place(so_far, shape, ema, me, chip, core, pieces):
    rows, width = shape
    columns = width // 2
    cols = columns // CORES
    ema_rows = ema.shape[0]
    where = jnp.stack([jnp.int32(x) for x in (me, chip, core, *(block for block, _, _ in pieces))])
    values = [x for _, mine, theirs in pieces for x in (mine, theirs)]

    def kernel(where_ref, ema_ref, *refs):
        full_out, ema_out, near, ema_near, new_near, sems = refs[-6:]
        here = pl.ds(pl.multiple_of(where_ref[1] * columns, LANES), columns)
        load = pltpu.make_async_copy(ema_ref.at[:, here], ema_near, sems.at[0])
        load.start()
        stores = []
        for k in range(len(pieces)):
            mine, theirs = refs[2 * k], refs[2 * k + 1]
            at = pl.ds(pl.multiple_of(where_ref[3 + k] * mine.shape[0], 16), mine.shape[0])

            @pl.when(where_ref[2] == 0)
            def _():
                near[at, :cols] = mine[...]
                near[at, cols:] = theirs[...]

            @pl.when(where_ref[2] != 0)
            def _():
                near[at, :cols] = theirs[...]
                near[at, cols:] = mine[...]

            stores.append(pltpu.make_async_copy(near.at[at, :], full_out.at[at, here], sems.at[2 + k]))
            stores[-1].start()
        load.wait()
        mine_rows = near[pl.ds(pl.multiple_of(where_ref[0] * ema_rows, 16), ema_rows), :]
        new_near[...] = 0.9 * ema_near[...] + 0.1 * widen(mine_rows)
        stores.append(pltpu.make_async_copy(new_near, ema_out.at[:, here], sems.at[1]))
        stores[-1].start()
        for store in stores:
            store.wait()

    far = pl.BlockSpec(memory_space=pltpu.HBM)
    return pl.pallas_call(
        kernel,
        in_specs=[pl.BlockSpec(memory_space=pltpu.SMEM), far]
        + [pl.BlockSpec(memory_space=pltpu.VMEM)] * len(values)
        + [far] * len(so_far),
        out_specs=[far, far],
        out_shape=[jax.ShapeDtypeStruct(shape, jnp.bfloat16), jax.ShapeDtypeStruct(ema.shape, jnp.float32)],
        input_output_aliases={2 + len(values) + i: i for i in range(len(so_far))},
        scratch_shapes=[
            pltpu.VMEM((rows, columns), jnp.bfloat16),
            pltpu.VMEM((ema_rows, columns), jnp.float32),
            pltpu.VMEM((ema_rows, columns), jnp.float32),
            pltpu.SemaphoreType.DMA((2 + len(pieces),)),
        ],
        cost_estimate=SMALL,
        compiler_params=PARAMS,
    )(where, ema, *values, *so_far)


def body(grad_proj, grad_conv, param_proj, m_proj, v_proj, ema_proj, param_conv, m_conv, v_conv):
    reps, owners = lax.axis_size("rep"), lax.axis_size("dp")
    replica_count = reps * owners
    chips = owners // CORES
    rows, cols = param_proj.shape
    shape = (rows, cols * owners)
    me = lax.axis_index("dp")
    chip, core = me // CORES, me % CORES
    rep = lax.axis_index("rep")
    part_rows = rows // CHUNKS
    aligned = cols % LANES == 0 and part_rows % 16 == 0
    line = reps == 4

    def core_swap(x):
        return exchange(x, "dp", 1)

    def chip_shift(x, off):
        pairs = [
            (a * CORES + c, ((a + off) % chips) * CORES + c) for a in range(chips) for c in range(CORES)
        ]
        return lax.ppermute(x, "dp", pairs)

    def chunk(x, i):
        return x[i * part_rows : (i + 1) * part_rows]

    odd = rep % 2 == 1

    def either(values):
        return jnp.where(odd, values[1], values[0])

    scale = 1.0 / max(1, 2 ** math.ceil(math.log2(replica_count / F16_SAFE_REPLICAS)))
    inverse = 1.0 / (replica_count * scale)
    grad = grad_proj[0]

    def scaled(x):
        return x * scale if scale != 1.0 else x

    def block(owner_chip, owner_core, i):
        start = i * part_rows
        if owners != 4:
            owner = owner_chip * CORES + owner_core
            return scaled(lax.dynamic_slice(grad, (start, owner * cols), (part_rows, cols)))
        a, b, c, d = (grad[start : start + part_rows, n * cols : (n + 1) * cols] for n in range(owners))
        return scaled(jnp.where(owner_chip == 0, jnp.where(owner_core == 0, a, b), jnp.where(owner_core == 0, c, d)))

    targets = [(chip + off) % chips for off in (*range(1, chips), 0)]
    own = chips - 1
    gifts = {}

    def give(n, i, core):
        gifts[n, i] = core_swap(narrow(block(targets[n], 1 - core, i)))

    def chip_sum(n, i):
        return block(targets[n], core, i) + widen(gifts[n, i])

    for n in range(own):
        give(n, 0, core)
    outgoing = {(n, 0): narrow(chip_sum(n, 0)) for n in range(own)}
    later_core = core
    give(own, 0, later_core)
    for i in range(1, CHUNKS):
        for n in range(chips):
            give(n, i, later_core)

    avgs, squares = [None] * CHUNKS, [None] * CHUNKS
    sums, halves, totals = {}, {}, {}
    is_end = (rep == 0) | (rep == 3)
    conv_steps = [*steps_of("rep"), *steps_of("dp")]
    conv_sum = grad_conv[0]

    def average_of(total):
        return widen(total) * inverse

    def square_of(total):
        value = average_of(total)
        return jnp.sum(value * value, axis=0, keepdims=True)

    moving, own_sums = {}, {}

    def chip_sum_after(n, i, payloads):
        if i > 1:
            gifts[n, i] = together(gifts[n, i], *payloads)[0]
        total = chip_sum(n, i)
        return total if n == own else narrow(total)

    rounds = CHUNKS + 2 if line else CHUNKS
    for r in range(rounds + 1):
        names = list(moving)
        there = dict(zip(names, together(*[moving[k] for k in names]))) if names else {}
        moving, waiting = {}, {}
        for k, value in there.items():
            if k[0] == "own":
                own_sums[k[1]] = value
            elif k[0] == "average":
                avgs[k[1]] = value
            elif k[0] == "square":
                squares[k[1]] = value
            elif k[0] == "outgoing":
                outgoing[k[1:]] = value

        if 0 <= r - 1 < CHUNKS:
            total = own_sums[r - 1]
            for n in range(own):
                total = total + widen(there["chips", n])
            sums[r - 1] = narrow(total) if line else lax.psum(total, "rep")
        if ("pair", 0) in there:
            i = r - 2
            if i < CHUNKS:
                halves[i] = narrow(widen(sums[i]) + widen(there["pair", 0]))
            if i >= 2:
                waiting["average", i - 2] = average_of(jnp.where(is_end, there["pair", 0], totals[i - 2]))
        if ("middle", 0) in there:
            totals[r - 3] = narrow(widen(halves[r - 3]) + widen(there["middle", 0]))
            if r < rounds:
                waiting["square", r - 3] = square_of(totals[r - 3])
            else:
                squares[r - 3] = square_of(together(totals[r - 3])[0])
        if ("conv", 0) in there:
            conv_sum = there["own conv", 0] + there["conv", 0]

        payloads = []
        if line and 0 <= r - 2 < CHUNKS:
            payloads.append(halves[r - 2])
            moving["middle", 0] = lax.ppermute(halves[r - 2], "rep", [(1, 2), (2, 1)])
        if r < CHUNKS:
            for n in range(own):
                payloads.append(outgoing[n, r])
                moving["chips", n] = chip_shift(payloads[-1], n + 1)
        i = r - 1
        if line and 0 <= i < CHUNKS + 2:
            if i < 2:
                payload = sums[i]
            elif i < CHUNKS:
                payload = jnp.where(is_end, sums[i], totals[i - 2])
            else:
                payload = totals[i - 2]
            payloads.append(payload)
            moving["pair", 0] = lax.ppermute(payload, "rep", [(0, 1), (1, 0), (2, 3), (3, 2)])
        if r < CHUNKS:
            if r + 1 < CHUNKS:
                for n in range(own):
                    waiting["outgoing", n, r + 1] = chip_sum_after(n, r + 1, payloads)
            waiting["own", r] = chip_sum_after(own, r, payloads)
        if conv_steps and payloads:
            sent, *_ = together(conv_sum, *payloads, *(waiting[k] for k in waiting if k[0] == "outgoing"))
            moving["own conv", 0] = sent
            moving["conv", 0] = exchange(sent, *conv_steps.pop(0))
        moving.update(waiting)

    if not line:
        avgs = [average_of(sums[i]) for i in range(CHUNKS)]
        squares = [square_of(sums[i]) for i in range(CHUNKS)]
    for step in conv_steps:
        conv_sum = conv_sum + exchange(conv_sum, *step)
    conv_avg = conv_sum / replica_count
    conv_square = jnp.sum(conv_avg * conv_avg)

    square = sum(squares[1:], squares[0])
    square = square + jnp.where(me == 0, conv_square, 0.0) * (lax.broadcasted_iota(jnp.int32, square.shape, 1) == 0)
    hops = [*steps_of("dp"), *steps_of("tensor")]
    for step in hops if not line else hops[:-1]:
        square = square + exchange(square, *step)
    if line:
        size, step = lax.axis_size("tensor"), hops[-1][1]
        across = [(a * size + t, (a ^ 1) * size + (t ^ step)) for a in range(reps) for t in range(size)]
        theirs = lax.ppermute(square, ("rep", "tensor"), across)
        inner, other = exchange(square, "rep", 1), exchange(square, *hops[-1])
        square = jnp.where(is_end, inner, square) + jnp.where(is_end, theirs, other)
        arrived = moving["pair", 0]
        for n in range(CHUNKS - 1):
            if avgs[n] is None:
                avgs[n] = moving["average", n]
    clip_factor = clip_from(jnp.sum(square, keepdims=True))

    def last_average(after):
        if not line:
            return avgs[-1]
        return average_of(jnp.where(is_end, together(arrived, after)[0], totals[CHUNKS - 1]))

    if not (aligned and chips == 2 and reps % 2 == 0 and CHUNKS == 3):
        avgs[-1] = last_average(clip_factor)
        results = adamw_step(param_proj, m_proj, v_proj, clip_factor * jnp.concatenate(avgs))
        weights = results[0].astype(jnp.bfloat16)
        full = jnp.zeros(shape, jnp.bfloat16)
        for piece, owner in ((weights, me), (core_swap(weights), me ^ 1)):
            full = lax.dynamic_update_slice(full, piece, (0, owner * cols))
        for off in range(1, chips):
            got = chip_shift(weights, off)
            from_chip = (chip - off) % chips
            for piece, owner in ((got, from_chip * CORES + core), (core_swap(got), from_chip * CORES + 1 - core)):
                full = lax.dynamic_update_slice(full, piece, (0, owner * cols))
        conv_results = adamw_step(param_conv, m_conv, v_conv, clip_factor * conv_avg)
        ema_count = ema_proj.shape[0]
        row_block = lax.dynamic_slice_in_dim(full, me * ema_count, ema_count, 0)
        return (*results, 0.9 * ema_proj + 0.1 * widen(row_block), full, *conv_results)

    g = either(avgs)
    start = jnp.where(odd, part_rows, 0)
    p, m, v = (lax.dynamic_slice(x, (start, 0), (part_rows, cols)) for x in (param_proj, m_proj, v_proj))
    first = adamw_step(p, m, v, clip_factor * g)[0].astype(jnp.bfloat16)
    got_first = chip_shift(first, 1)
    avgs[-1] = last_average(first)
    *results, weights, third = step_state(avgs, clip_factor, param_proj, m_proj, v_proj)
    weights, got_first, third = together(weights, got_first, third)

    got_third = chip_shift(third, 1)
    got_second = exchange(got_first, "rep", 1)
    got_first_other = core_swap(got_first)
    so_far = place([], shape, ema_proj, me, chip, core, [(0, weights, core_swap(weights))])
    clip, _ = together(clip_factor, so_far[0])
    conv_results = adamw_step(param_conv, m_conv, v_conv, clip * conv_avg)
    got_third, got_second, *_ = together(got_third, got_second, *so_far, conv_results[0])
    first_block = jnp.where(odd, 1, 0)
    pieces = [
        (first_block, got_first, got_first_other),
        (1 - first_block, got_second, core_swap(got_second)),
        (2, got_third, core_swap(got_third)),
    ]
    full, new_ema = place(so_far, shape, ema_proj, me, 1 - chip, core, pieces)
    return (*results, new_ema, full, *conv_results)


def solution(mesh):
    in_specs = (
        P(("rep", "dp"), "tensor", None),
        P(("rep", "dp"), None, "tensor"),
        P("tensor", "dp"),
        P("tensor", "dp"),
        P("tensor", "dp"),
        P(("tensor", "dp"), None),
        P(None, "tensor"),
        P(None, "tensor"),
        P(None, "tensor"),
    )
    out_specs = (
        P("tensor", "dp"),
        P("tensor", "dp"),
        P("tensor", "dp"),
        P(("tensor", "dp"), None),
        P("tensor", None),
        P(None, "tensor"),
        P(None, "tensor"),
        P(None, "tensor"),
    )
    return jax.shard_map(body, mesh=mesh, in_specs=in_specs, out_specs=out_specs, check_vma=False)
```

```python
import math

import jax
import jax.numpy as jnp
from jax import lax
from jax.experimental import pallas as pl
from jax.experimental.pallas import tpu as pltpu
from jax.sharding import PartitionSpec as P

D = 1536
INNER = 3072
CONV = 3328
KCONV = 4

CORES = 2
CHUNKS = 3
LANES = 128
F16_SAFE_REPLICAS = 16
PARAMS = pltpu.CompilerParams(vmem_limit_bytes=16 * 2**20)
SMALL = pl.CostEstimate(flops=1, bytes_accessed=1024, transcendentals=1)


def adamw_step(param_in, first_in, second_in, grad_in):
    first_out = 0.9 * first_in + 0.1 * grad_in
    second_out = 0.95 * second_in + 0.05 * grad_in * grad_in
    bias_one = 1.0 - 0.9**10
    bias_two = 1.0 - 0.95**10
    update = first_out / bias_one / (jnp.sqrt(second_out / bias_two) + 1e-08)
    param_out = param_in - 0.25 * (update + 0.1 * param_in)
    return (param_out, first_out, second_out)


def clip_from(square_sum):
    clip_limit = 0.5 * math.sqrt(INNER * D + KCONV * CONV)
    return jnp.minimum(1.0, clip_limit / (jnp.sqrt(square_sum) + 1e-06))


def exchange(value, axis, step):
    return lax.ppermute(value, axis, [(i, i ^ step) for i in range(lax.axis_size(axis))])


def steps_of(axis, first=1):
    steps = []
    while first < lax.axis_size(axis):
        steps.append((axis, first))
        first *= 2
    return steps


def widen(x):
    return x.astype(jnp.float32)


def narrow(x):
    return x.astype(jnp.float16)


def together(*values):
    return lax.optimization_barrier(values)


def step_state(avgs, clip, param, first, second):
    rows, cols = param.shape
    chunks = len(avgs)
    part = rows // chunks

    def kernel(clip_ref, *refs):
        avg_refs, old_refs, new_refs = refs[:chunks], refs[chunks : chunks + 3], refs[chunks + 3 : chunks + 6]
        w_out, last_out, near, sems = refs[chunks + 6 :]
        loads, stores = [], []
        for k in range(chunks):
            at = pl.ds(k * part, part)
            for n in range(3):
                loads.append(pltpu.make_async_copy(old_refs[n].at[at, :], near.at[n, at, :], sems.at[3 * k + n]))
                loads[-1].start()
        for k in range(chunks):
            at = slice(k * part, (k + 1) * part)
            for load in loads[3 * k : 3 * k + 3]:
                load.wait()
            new = adamw_step(near[0, at], near[1, at], near[2, at], clip_ref[0, 0] * avg_refs[k][...])
            for n in range(3):
                near[n, at] = new[n]
                here = pl.ds(k * part, part)
                sem = sems.at[3 * (chunks + k) + n]
                stores.append(pltpu.make_async_copy(near.at[n, here, :], new_refs[n].at[here, :], sem))
                stores[-1].start()
            w_out[at, :] = new[0].astype(jnp.bfloat16)
            if k == chunks - 1:
                last_out[...] = new[0].astype(jnp.bfloat16)
        for store in stores:
            store.wait()

    far, close = pl.BlockSpec(memory_space=pltpu.HBM), pl.BlockSpec(memory_space=pltpu.VMEM)
    whole = jax.ShapeDtypeStruct((rows, cols), jnp.float32)
    return pl.pallas_call(
        kernel,
        in_specs=[pl.BlockSpec(memory_space=pltpu.SMEM)] + [close] * chunks + [far] * 3,
        out_specs=[far] * 3 + [close] * 2,
        out_shape=[whole, whole, whole]
        + [jax.ShapeDtypeStruct((rows, cols), jnp.bfloat16), jax.ShapeDtypeStruct((part, cols), jnp.bfloat16)],
        scratch_shapes=[pltpu.VMEM((3, rows, cols), jnp.float32), pltpu.SemaphoreType.DMA((6 * chunks,))],
        cost_estimate=SMALL,
        compiler_params=pltpu.CompilerParams(vmem_limit_bytes=48 * 2**20),
    )(clip, *avgs, param, first, second)


def place(so_far, shape, ema, rest, me, chip, core, pieces, written):
    rows, width = shape
    columns = width // 2
    cols = columns // CORES
    ema_rows = shape[0] // (width // cols)
    where = jnp.stack([jnp.int32(x) for x in (me, chip, core, *(block for block, _, _ in pieces))])
    values = [x for _, mine, theirs in pieces for x in (mine, theirs)]
    starts = rest is None

    def kernel(where_ref, old_ref, *refs):
        outs = 3 if starts else 2
        scratch = refs[-3:] if not starts else refs[-4:]
        full_out, ema_out = refs[-len(scratch) - outs : -len(scratch)][:2]
        near, new_near, sems = scratch[-3:]
        here = pl.ds(pl.multiple_of(where_ref[1] * columns, LANES), columns)
        if starts:
            rest_out, old_near = refs[-5], refs[-4]
            load = pltpu.make_async_copy(old_ref, old_near, sems.at[0])
            load.start()
        stores = []
        for k in range(len(pieces)):
            mine, theirs = refs[2 * k], refs[2 * k + 1]
            at = pl.ds(pl.multiple_of(where_ref[3 + k] * mine.shape[0], 16), mine.shape[0])

            @pl.when(where_ref[2] == 0)
            def _():
                near[at, :cols] = mine[...]
                near[at, cols:] = theirs[...]

            @pl.when(where_ref[2] != 0)
            def _():
                near[at, :cols] = theirs[...]
                near[at, cols:] = mine[...]

            if k >= written:
                stores.append(pltpu.make_async_copy(near.at[at, :], full_out.at[at, here], sems.at[2 + k]))
                stores[-1].start()
        mine_rows = near[pl.ds(pl.multiple_of(where_ref[0] * ema_rows, 16), ema_rows), :]
        if starts:
            load.wait()
            there = pl.ds(pl.multiple_of((1 - where_ref[1]) * columns, LANES), columns)
            new_near[...] = 0.9 * old_near[:, here] + 0.1 * widen(mine_rows)
            rest_out[...] = 0.9 * old_near[:, there]
        else:
            new_near[...] = old_ref[...] + 0.1 * widen(mine_rows)
        stores.append(pltpu.make_async_copy(new_near, ema_out.at[:, here], sems.at[1]))
        stores[-1].start()
        for store in stores:
            store.wait()

    far = pl.BlockSpec(memory_space=pltpu.HBM)
    close = pl.BlockSpec(memory_space=pltpu.VMEM)
    old = jax.ShapeDtypeStruct((ema_rows, width), jnp.float32)
    half = jax.ShapeDtypeStruct((ema_rows, columns), jnp.float32)
    return pl.pallas_call(
        kernel,
        in_specs=[pl.BlockSpec(memory_space=pltpu.SMEM), far if starts else close]
        + [close] * len(values)
        + [far] * len(so_far),
        out_specs=[far, far] + [close] * starts,
        out_shape=[jax.ShapeDtypeStruct(shape, jnp.bfloat16), old] + [half] * starts,
        input_output_aliases={2 + len(values) + i: i for i in range(len(so_far))},
        scratch_shapes=[pltpu.VMEM(old.shape, jnp.float32)] * starts
        + [
            pltpu.VMEM((rows, columns), jnp.bfloat16),
            pltpu.VMEM(half.shape, jnp.float32),
            pltpu.SemaphoreType.DMA((2 + len(pieces),)),
        ],
        cost_estimate=SMALL,
        compiler_params=pltpu.CompilerParams(vmem_limit_bytes=40 * 2**20),
    )(where, ema if starts else rest, *values, *so_far)


def body(grad_proj, grad_conv, param_proj, m_proj, v_proj, ema_proj, param_conv, m_conv, v_conv):
    reps, owners = lax.axis_size("rep"), lax.axis_size("dp")
    replica_count = reps * owners
    chips = owners // CORES
    rows, cols = param_proj.shape
    shape = (rows, cols * owners)
    me = lax.axis_index("dp")
    chip, core = me // CORES, me % CORES
    rep = lax.axis_index("rep")
    part_rows = rows // CHUNKS
    aligned = cols % LANES == 0 and part_rows % 16 == 0
    line = reps == 4

    def core_swap(x):
        return exchange(x, "dp", 1)

    def chip_shift(x, off):
        pairs = [
            (a * CORES + c, ((a + off) % chips) * CORES + c) for a in range(chips) for c in range(CORES)
        ]
        return lax.ppermute(x, "dp", pairs)

    def chunk(x, i):
        return x[i * part_rows : (i + 1) * part_rows]

    odd = rep % 2 == 1

    def either(values):
        return jnp.where(odd, values[1], values[0])

    scale = 1.0 / max(1, 2 ** math.ceil(math.log2(replica_count / F16_SAFE_REPLICAS)))
    inverse = 1.0 / (replica_count * scale)
    grad = grad_proj[0]

    def scaled(x):
        return x * scale if scale != 1.0 else x

    def block(owner_chip, owner_core, i):
        start = i * part_rows
        if owners != 4:
            owner = owner_chip * CORES + owner_core
            return scaled(lax.dynamic_slice(grad, (start, owner * cols), (part_rows, cols)))
        a, b, c, d = (grad[start : start + part_rows, n * cols : (n + 1) * cols] for n in range(owners))
        return scaled(jnp.where(owner_chip == 0, jnp.where(owner_core == 0, a, b), jnp.where(owner_core == 0, c, d)))

    targets = [(chip + off) % chips for off in (*range(1, chips), 0)]
    own = chips - 1
    gifts = {}

    def give(n, i, core):
        gifts[n, i] = core_swap(narrow(block(targets[n], 1 - core, i)))

    def chip_sum(n, i):
        return block(targets[n], core, i) + widen(gifts[n, i])

    for n in range(own):
        give(n, 0, core)
    outgoing = {(n, 0): narrow(chip_sum(n, 0)) for n in range(own)}
    later_core = core
    give(own, 0, later_core)
    for i in range(1, CHUNKS):
        for n in range(chips):
            give(n, i, later_core)

    avgs, squares = [None] * CHUNKS, [None] * CHUNKS
    sums, halves, totals = {}, {}, {}
    is_end = (rep == 0) | (rep == 3)
    conv_steps = [*steps_of("rep"), *steps_of("dp")]
    conv_sum = grad_conv[0]

    def average_of(total):
        return widen(total) * inverse

    def square_of(total):
        value = average_of(total)
        return jnp.sum(value * value, axis=0, keepdims=True)

    moving, own_sums = {}, {}

    def chip_sum_after(n, i, payloads):
        if i > 1:
            gifts[n, i] = together(gifts[n, i], *payloads)[0]
        total = chip_sum(n, i)
        return total if n == own else narrow(total)

    rounds = CHUNKS + 2 if line else CHUNKS
    for r in range(rounds + 1):
        names = list(moving)
        there = dict(zip(names, together(*[moving[k] for k in names]))) if names else {}
        moving, waiting = {}, {}
        for k, value in there.items():
            if k[0] == "own":
                own_sums[k[1]] = value
            elif k[0] == "average":
                avgs[k[1]] = value
            elif k[0] == "square":
                squares[k[1]] = value
            elif k[0] == "outgoing":
                outgoing[k[1:]] = value

        if 0 <= r - 1 < CHUNKS:
            total = own_sums[r - 1]
            for n in range(own):
                total = total + widen(there["chips", n])
            sums[r - 1] = narrow(total) if line else lax.psum(total, "rep")
        if ("pair", 0) in there:
            i = r - 2
            if i < CHUNKS:
                halves[i] = narrow(widen(sums[i]) + widen(there["pair", 0]))
            if i >= 2:
                waiting["average", i - 2] = average_of(jnp.where(is_end, there["pair", 0], totals[i - 2]))
        if ("middle", 0) in there:
            totals[r - 3] = narrow(widen(halves[r - 3]) + widen(there["middle", 0]))
            if r < rounds:
                waiting["square", r - 3] = square_of(totals[r - 3])
            else:
                squares[r - 3] = square_of(together(totals[r - 3])[0])
        if ("conv", 0) in there:
            conv_sum = there["own conv", 0] + there["conv", 0]

        payloads = []
        if line and 0 <= r - 2 < CHUNKS:
            payloads.append(halves[r - 2])
            moving["middle", 0] = lax.ppermute(halves[r - 2], "rep", [(1, 2), (2, 1)])
        if r < CHUNKS:
            for n in range(own):
                payloads.append(outgoing[n, r])
                moving["chips", n] = chip_shift(payloads[-1], n + 1)
        i = r - 1
        if line and 0 <= i < CHUNKS + 2:
            if i < 2:
                payload = sums[i]
            elif i < CHUNKS:
                payload = jnp.where(is_end, sums[i], totals[i - 2])
            else:
                payload = totals[i - 2]
            payloads.append(payload)
            moving["pair", 0] = lax.ppermute(payload, "rep", [(0, 1), (1, 0), (2, 3), (3, 2)])
        if r < CHUNKS:
            if r + 1 < CHUNKS:
                for n in range(own):
                    waiting["outgoing", n, r + 1] = chip_sum_after(n, r + 1, payloads)
            waiting["own", r] = chip_sum_after(own, r, payloads)
        if conv_steps and payloads:
            sent, *_ = together(conv_sum, *payloads, *(waiting[k] for k in waiting if k[0] == "outgoing"))
            moving["own conv", 0] = sent
            moving["conv", 0] = exchange(sent, *conv_steps.pop(0))
        moving.update(waiting)

    if not line:
        avgs = [average_of(sums[i]) for i in range(CHUNKS)]
        squares = [square_of(sums[i]) for i in range(CHUNKS)]
    for step in conv_steps:
        conv_sum = conv_sum + exchange(conv_sum, *step)
    conv_avg = conv_sum / replica_count
    conv_square = jnp.sum(conv_avg * conv_avg)

    square = sum(squares[1:], squares[0])
    square = square + jnp.where(me == 0, conv_square, 0.0) * (lax.broadcasted_iota(jnp.int32, square.shape, 1) == 0)
    hops = [*steps_of("dp"), *steps_of("tensor")]
    for step in hops if not line else hops[:-1]:
        square = square + exchange(square, *step)
    if line:
        size, step = lax.axis_size("tensor"), hops[-1][1]
        across = [(a * size + t, (a ^ 1) * size + (t ^ step)) for a in range(reps) for t in range(size)]
        theirs = lax.ppermute(square, ("rep", "tensor"), across)
        inner, other = exchange(square, "rep", 1), exchange(square, *hops[-1])
        square = jnp.where(is_end, inner, square) + jnp.where(is_end, theirs, other)
        arrived = moving["pair", 0]
        for n in range(CHUNKS - 1):
            if avgs[n] is None:
                avgs[n] = moving["average", n]
    clip_factor = clip_from(jnp.sum(square, keepdims=True))

    def last_average(after):
        if not line:
            return avgs[-1]
        return average_of(jnp.where(is_end, together(arrived, after)[0], totals[CHUNKS - 1]))

    if not (aligned and chips == 2 and reps % 2 == 0 and CHUNKS == 3):
        avgs[-1] = last_average(clip_factor)
        results = adamw_step(param_proj, m_proj, v_proj, clip_factor * jnp.concatenate(avgs))
        weights = results[0].astype(jnp.bfloat16)
        full = jnp.zeros(shape, jnp.bfloat16)
        for piece, owner in ((weights, me), (core_swap(weights), me ^ 1)):
            full = lax.dynamic_update_slice(full, piece, (0, owner * cols))
        for off in range(1, chips):
            got = chip_shift(weights, off)
            from_chip = (chip - off) % chips
            for piece, owner in ((got, from_chip * CORES + core), (core_swap(got), from_chip * CORES + 1 - core)):
                full = lax.dynamic_update_slice(full, piece, (0, owner * cols))
        conv_results = adamw_step(param_conv, m_conv, v_conv, clip_factor * conv_avg)
        ema_count = ema_proj.shape[0]
        row_block = lax.dynamic_slice_in_dim(full, me * ema_count, ema_count, 0)
        return (*results, 0.9 * ema_proj + 0.1 * widen(row_block), full, *conv_results)

    g = either(avgs)
    start = jnp.where(odd, part_rows, 0)
    p, m, v = (lax.dynamic_slice(x, (start, 0), (part_rows, cols)) for x in (param_proj, m_proj, v_proj))
    first = adamw_step(p, m, v, clip_factor * g)[0].astype(jnp.bfloat16)
    got_first = chip_shift(first, 1)
    avgs[-1] = last_average(first)
    *results, weights, third = step_state(avgs, clip_factor, param_proj, m_proj, v_proj)
    weights, got_first, third = together(weights, got_first, third)

    got_third = chip_shift(third, 1)
    got_second = exchange(got_first, "rep", 1)
    got_first_other = core_swap(got_first)
    *so_far, rest = place([], shape, ema_proj, None, me, chip, core, [(0, weights, core_swap(weights))], 0)
    clip, _ = together(clip_factor, so_far[0])
    conv_results = adamw_step(param_conv, m_conv, v_conv, clip * conv_avg)
    got_second, *_ = together(got_second, *so_far, conv_results[0])
    got_second_other = core_swap(got_second)
    got_third, _ = together(got_third, got_second)
    first_block = jnp.where(odd, 1, 0)
    pieces = [
        (first_block, got_first, got_first_other),
        (1 - first_block, got_second, got_second_other),
        (2, got_third, core_swap(got_third)),
    ]
    full, new_ema = place(so_far, shape, None, rest, me, 1 - chip, core, pieces, 0)
    return (*results, new_ema, full, *conv_results)


def solution(mesh):
    in_specs = (
        P(("rep", "dp"), "tensor", None),
        P(("rep", "dp"), None, "tensor"),
        P("tensor", "dp"),
        P("tensor", "dp"),
        P("tensor", "dp"),
        P(("tensor", "dp"), None),
        P(None, "tensor"),
        P(None, "tensor"),
        P(None, "tensor"),
    )
    out_specs = (
        P("tensor", "dp"),
        P("tensor", "dp"),
        P("tensor", "dp"),
        P(("tensor", "dp"), None),
        P("tensor", None),
        P(None, "tensor"),
        P(None, "tensor"),
        P(None, "tensor"),
    )
    return jax.shard_map(body, mesh=mesh, in_specs=in_specs, out_specs=out_specs, check_vma=False)
```

```python
import math

import jax
import jax.numpy as jnp
from jax import lax
from jax.experimental import pallas as pl
from jax.experimental.pallas import tpu as pltpu
from jax.sharding import PartitionSpec as P

D = 1536
INNER = 3072
CONV = 3328
KCONV = 4

CORES = 2
CHUNKS = 3
LANES = 128
F16_SAFE_REPLICAS = 16
PARAMS = pltpu.CompilerParams(vmem_limit_bytes=16 * 2**20)
SMALL = pl.CostEstimate(flops=1, bytes_accessed=1024, transcendentals=1)


def adamw_step(param_in, first_in, second_in, grad_in):
    first_out = 0.9 * first_in + 0.1 * grad_in
    second_out = 0.95 * second_in + 0.05 * grad_in * grad_in
    bias_one = 1.0 - 0.9**10
    bias_two = 1.0 - 0.95**10
    update = first_out / bias_one / (jnp.sqrt(second_out / bias_two) + 1e-08)
    param_out = param_in - 0.25 * (update + 0.1 * param_in)
    return (param_out, first_out, second_out)


def clip_from(square_sum):
    clip_limit = 0.5 * math.sqrt(INNER * D + KCONV * CONV)
    return jnp.minimum(1.0, clip_limit / (jnp.sqrt(square_sum) + 1e-06))


def exchange(value, axis, step):
    return lax.ppermute(value, axis, [(i, i ^ step) for i in range(lax.axis_size(axis))])


def steps_of(axis, first=1):
    steps = []
    while first < lax.axis_size(axis):
        steps.append((axis, first))
        first *= 2
    return steps


def widen(x):
    return x.astype(jnp.float32)


def narrow(x):
    return x.astype(jnp.float16)


def together(*values):
    return lax.optimization_barrier(values)


def step_state(avgs, clip, param, first, second):
    rows, cols = param.shape
    chunks = len(avgs)
    part = rows // chunks

    def kernel(clip_ref, *refs):
        avg_refs, old_refs, new_refs = refs[:chunks], refs[chunks : chunks + 3], refs[chunks + 3 : chunks + 6]
        w_out, last_out, near, sems = refs[chunks + 6 :]
        loads, stores = [], []
        for k in range(chunks):
            at = pl.ds(k * part, part)
            for n in range(3):
                loads.append(pltpu.make_async_copy(old_refs[n].at[at, :], near.at[n, at, :], sems.at[3 * k + n]))
                loads[-1].start()
        for k in range(chunks):
            at = slice(k * part, (k + 1) * part)
            for load in loads[3 * k : 3 * k + 3]:
                load.wait()
            new = adamw_step(near[0, at], near[1, at], near[2, at], clip_ref[0, 0] * avg_refs[k][...])
            for n in range(3):
                near[n, at] = new[n]
                here = pl.ds(k * part, part)
                sem = sems.at[3 * (chunks + k) + n]
                stores.append(pltpu.make_async_copy(near.at[n, here, :], new_refs[n].at[here, :], sem))
                stores[-1].start()
            w_out[at, :] = new[0].astype(jnp.bfloat16)
            if k == chunks - 1:
                last_out[...] = new[0].astype(jnp.bfloat16)
        for store in stores:
            store.wait()

    far, close = pl.BlockSpec(memory_space=pltpu.HBM), pl.BlockSpec(memory_space=pltpu.VMEM)
    whole = jax.ShapeDtypeStruct((rows, cols), jnp.float32)
    return pl.pallas_call(
        kernel,
        in_specs=[pl.BlockSpec(memory_space=pltpu.SMEM)] + [close] * chunks + [far] * 3,
        out_specs=[far] * 3 + [close] * 2,
        out_shape=[whole, whole, whole]
        + [jax.ShapeDtypeStruct((rows, cols), jnp.bfloat16), jax.ShapeDtypeStruct((part, cols), jnp.bfloat16)],
        scratch_shapes=[pltpu.VMEM((3, rows, cols), jnp.float32), pltpu.SemaphoreType.DMA((6 * chunks,))],
        cost_estimate=SMALL,
        compiler_params=pltpu.CompilerParams(vmem_limit_bytes=48 * 2**20),
    )(clip, *avgs, param, first, second)


def place(so_far, shape, ema, rest, me, chip, core, pieces, written):
    rows, width = shape
    columns = width // 2
    cols = columns // CORES
    ema_rows = shape[0] // (width // cols)
    where = jnp.stack([jnp.int32(x) for x in (me, chip, core, *(block for block, _, _ in pieces))])
    values = [x for _, mine, theirs in pieces for x in (mine, theirs)]
    starts = rest is None

    def kernel(where_ref, old_ref, *refs):
        outs = 3 if starts else 2
        scratch = refs[-3:] if not starts else refs[-4:]
        full_out, ema_out = refs[-len(scratch) - outs : -len(scratch)][:2]
        near, new_near, sems = scratch[-3:]
        here = pl.ds(pl.multiple_of(where_ref[1] * columns, LANES), columns)
        if starts:
            rest_out, old_near = refs[-5], refs[-4]
            load = pltpu.make_async_copy(old_ref, old_near, sems.at[0])
            load.start()
        stores = []
        for k in range(len(pieces)):
            mine, theirs = refs[2 * k], refs[2 * k + 1]
            at = pl.ds(pl.multiple_of(where_ref[3 + k] * mine.shape[0], 16), mine.shape[0])

            @pl.when(where_ref[2] == 0)
            def _():
                near[at, :cols] = mine[...]
                near[at, cols:] = theirs[...]

            @pl.when(where_ref[2] != 0)
            def _():
                near[at, :cols] = theirs[...]
                near[at, cols:] = mine[...]

            if k >= written:
                stores.append(pltpu.make_async_copy(near.at[at, :], full_out.at[at, here], sems.at[2 + k]))
                stores[-1].start()
        mine_rows = near[pl.ds(pl.multiple_of(where_ref[0] * ema_rows, 16), ema_rows), :]
        if starts:
            load.wait()
            there = pl.ds(pl.multiple_of((1 - where_ref[1]) * columns, LANES), columns)
            new_near[...] = 0.9 * old_near[:, here] + 0.1 * widen(mine_rows)
            rest_out[...] = 0.9 * old_near[:, there]
        else:
            new_near[...] = old_ref[...] + 0.1 * widen(mine_rows)
        stores.append(pltpu.make_async_copy(new_near, ema_out.at[:, here], sems.at[1]))
        stores[-1].start()
        for store in stores:
            store.wait()

    far = pl.BlockSpec(memory_space=pltpu.HBM)
    close = pl.BlockSpec(memory_space=pltpu.VMEM)
    old = jax.ShapeDtypeStruct((ema_rows, width), jnp.float32)
    half = jax.ShapeDtypeStruct((ema_rows, columns), jnp.float32)
    return pl.pallas_call(
        kernel,
        in_specs=[pl.BlockSpec(memory_space=pltpu.SMEM), far if starts else close]
        + [close] * len(values)
        + [far] * len(so_far),
        out_specs=[far, far] + [close] * starts,
        out_shape=[jax.ShapeDtypeStruct(shape, jnp.bfloat16), old] + [half] * starts,
        input_output_aliases={2 + len(values) + i: i for i in range(len(so_far))},
        scratch_shapes=[pltpu.VMEM(old.shape, jnp.float32)] * starts
        + [
            pltpu.VMEM((rows, columns), jnp.bfloat16),
            pltpu.VMEM(half.shape, jnp.float32),
            pltpu.SemaphoreType.DMA((2 + len(pieces),)),
        ],
        cost_estimate=SMALL,
        compiler_params=pltpu.CompilerParams(vmem_limit_bytes=40 * 2**20),
    )(where, ema if starts else rest, *values, *so_far)


def body(grad_proj, grad_conv, param_proj, m_proj, v_proj, ema_proj, param_conv, m_conv, v_conv):
    reps, owners = lax.axis_size("rep"), lax.axis_size("dp")
    replica_count = reps * owners
    chips = owners // CORES
    rows, cols = param_proj.shape
    shape = (rows, cols * owners)
    me = lax.axis_index("dp")
    chip, core = me // CORES, me % CORES
    rep = lax.axis_index("rep")
    part_rows = rows // CHUNKS
    aligned = cols % LANES == 0 and part_rows % 16 == 0
    line = reps == 4

    def core_swap(x):
        return exchange(x, "dp", 1)

    def chip_shift(x, off):
        pairs = [
            (a * CORES + c, ((a + off) % chips) * CORES + c) for a in range(chips) for c in range(CORES)
        ]
        return lax.ppermute(x, "dp", pairs)

    def chunk(x, i):
        return x[i * part_rows : (i + 1) * part_rows]

    odd = rep % 2 == 1

    def either(values):
        return jnp.where(odd, values[1], values[0])

    scale = 1.0 / max(1, 2 ** math.ceil(math.log2(replica_count / F16_SAFE_REPLICAS)))
    inverse = 1.0 / (replica_count * scale)
    grad = grad_proj[0]

    def scaled(x):
        return x * scale if scale != 1.0 else x

    def block(owner_chip, owner_core, i):
        start = i * part_rows
        if owners != 4:
            owner = owner_chip * CORES + owner_core
            return scaled(lax.dynamic_slice(grad, (start, owner * cols), (part_rows, cols)))
        a, b, c, d = (grad[start : start + part_rows, n * cols : (n + 1) * cols] for n in range(owners))
        return scaled(jnp.where(owner_chip == 0, jnp.where(owner_core == 0, a, b), jnp.where(owner_core == 0, c, d)))

    targets = [(chip + off) % chips for off in (*range(1, chips), 0)]
    own = chips - 1
    gifts = {}

    def give(n, i, core):
        gifts[n, i] = core_swap(narrow(block(targets[n], 1 - core, i)))

    def chip_sum(n, i):
        return block(targets[n], core, i) + widen(gifts[n, i])

    for n in range(own):
        give(n, 0, core)
    outgoing = {(n, 0): narrow(chip_sum(n, 0)) for n in range(own)}
    later_core = core
    give(own, 0, later_core)
    for i in range(1, CHUNKS):
        for n in range(chips):
            give(n, i, later_core)

    avgs, squares = [None] * CHUNKS, [None] * CHUNKS
    sums, halves, totals = {}, {}, {}
    is_end = (rep == 0) | (rep == 3)
    conv_steps = [*steps_of("rep"), *steps_of("dp")]
    conv_sum = grad_conv[0]

    def average_of(total):
        return widen(total) * inverse

    def square_of(total):
        value = average_of(total)
        return jnp.sum(value * value, axis=0, keepdims=True)

    moving, own_sums = {}, {}

    def chip_sum_after(n, i, payloads):
        if i > 1:
            gifts[n, i] = together(gifts[n, i], *payloads)[0]
        total = chip_sum(n, i)
        return total if n == own else narrow(total)

    rounds = CHUNKS + 2 if line else CHUNKS
    for r in range(rounds + 1):
        names = list(moving)
        there = dict(zip(names, together(*[moving[k] for k in names]))) if names else {}
        moving, waiting = {}, {}
        for k, value in there.items():
            if k[0] == "own":
                own_sums[k[1]] = value
            elif k[0] == "average":
                avgs[k[1]] = value
            elif k[0] == "square":
                squares[k[1]] = value
            elif k[0] == "outgoing":
                outgoing[k[1:]] = value

        if 0 <= r - 1 < CHUNKS:
            total = own_sums[r - 1]
            for n in range(own):
                total = total + widen(there["chips", n])
            sums[r - 1] = narrow(total) if line else lax.psum(total, "rep")
        if ("pair", 0) in there:
            i = r - 2
            if i < CHUNKS:
                halves[i] = narrow(widen(sums[i]) + widen(there["pair", 0]))
            if i >= 2:
                waiting["average", i - 2] = average_of(jnp.where(is_end, there["pair", 0], totals[i - 2]))
        if ("middle", 0) in there:
            totals[r - 3] = narrow(widen(halves[r - 3]) + widen(there["middle", 0]))
            if r < rounds:
                waiting["square", r - 3] = square_of(totals[r - 3])
            else:
                squares[r - 3] = square_of(together(totals[r - 3])[0])
        if ("conv", 0) in there:
            conv_sum = there["own conv", 0] + there["conv", 0]

        payloads = []
        if line and 0 <= r - 2 < CHUNKS:
            payloads.append(halves[r - 2])
            moving["middle", 0] = lax.ppermute(halves[r - 2], "rep", [(1, 2), (2, 1)])
        if r < CHUNKS:
            for n in range(own):
                payloads.append(outgoing[n, r])
                moving["chips", n] = chip_shift(payloads[-1], n + 1)
        i = r - 1
        if line and 0 <= i < CHUNKS + 2:
            if i < 2:
                payload = sums[i]
            elif i < CHUNKS:
                payload = jnp.where(is_end, sums[i], totals[i - 2])
            else:
                payload = totals[i - 2]
            payloads.append(payload)
            moving["pair", 0] = lax.ppermute(payload, "rep", [(0, 1), (1, 0), (2, 3), (3, 2)])
        if r < CHUNKS:
            if r + 1 < CHUNKS:
                for n in range(own):
                    waiting["outgoing", n, r + 1] = chip_sum_after(n, r + 1, payloads)
            waiting["own", r] = chip_sum_after(own, r, payloads)
        if conv_steps and payloads:
            sent, *_ = together(conv_sum, *payloads, *(waiting[k] for k in waiting if k[0] == "outgoing"))
            moving["own conv", 0] = sent
            moving["conv", 0] = exchange(sent, *conv_steps.pop(0))
        moving.update(waiting)

    if not line:
        avgs = [average_of(sums[i]) for i in range(CHUNKS)]
        squares = [square_of(sums[i]) for i in range(CHUNKS)]
    for step in conv_steps:
        conv_sum = conv_sum + exchange(conv_sum, *step)
    conv_avg = conv_sum / replica_count
    conv_square = jnp.sum(conv_avg * conv_avg)

    square = sum(squares[1:], squares[0])
    square = square + jnp.where(me == 0, conv_square, 0.0) * (lax.broadcasted_iota(jnp.int32, square.shape, 1) == 0)
    if square.shape[1] % LANES == 0:
        square = jnp.sum(square.reshape(-1, LANES), axis=0, keepdims=True)
    hops = [*steps_of("dp"), *steps_of("tensor")]
    for step in hops if not line else hops[:-1]:
        square = square + exchange(square, *step)
    if line:
        size, step = lax.axis_size("tensor"), hops[-1][1]
        across = [(a * size + t, (a ^ 1) * size + (t ^ step)) for a in range(reps) for t in range(size)]
        theirs = lax.ppermute(square, ("rep", "tensor"), across)
        inner, other = exchange(square, "rep", 1), exchange(square, *hops[-1])
        square = jnp.where(is_end, inner, square) + jnp.where(is_end, theirs, other)
        arrived = moving["pair", 0]
        for n in range(CHUNKS - 1):
            if avgs[n] is None:
                avgs[n] = moving["average", n]
    clip_factor = clip_from(jnp.sum(square, keepdims=True))

    def last_average(after):
        if not line:
            return avgs[-1]
        return average_of(jnp.where(is_end, together(arrived, after)[0], totals[CHUNKS - 1]))

    if not (aligned and chips == 2 and reps % 2 == 0 and CHUNKS == 3):
        avgs[-1] = last_average(clip_factor)
        results = adamw_step(param_proj, m_proj, v_proj, clip_factor * jnp.concatenate(avgs))
        weights = results[0].astype(jnp.bfloat16)
        full = jnp.zeros(shape, jnp.bfloat16)
        for piece, owner in ((weights, me), (core_swap(weights), me ^ 1)):
            full = lax.dynamic_update_slice(full, piece, (0, owner * cols))
        for off in range(1, chips):
            got = chip_shift(weights, off)
            from_chip = (chip - off) % chips
            for piece, owner in ((got, from_chip * CORES + core), (core_swap(got), from_chip * CORES + 1 - core)):
                full = lax.dynamic_update_slice(full, piece, (0, owner * cols))
        conv_results = adamw_step(param_conv, m_conv, v_conv, clip_factor * conv_avg)
        ema_count = ema_proj.shape[0]
        row_block = lax.dynamic_slice_in_dim(full, me * ema_count, ema_count, 0)
        return (*results, 0.9 * ema_proj + 0.1 * widen(row_block), full, *conv_results)

    g = either(avgs)
    start = jnp.where(odd, part_rows, 0)
    p, m, v = (lax.dynamic_slice(x, (start, 0), (part_rows, cols)) for x in (param_proj, m_proj, v_proj))
    first = adamw_step(p, m, v, clip_factor * g)[0].astype(jnp.bfloat16)
    got_first = chip_shift(first, 1)
    avgs[-1] = last_average(first)
    *results, weights, third = step_state(avgs, clip_factor, param_proj, m_proj, v_proj)
    weights, got_first = together(weights, got_first)

    got_third = chip_shift(third, 1)
    got_second = exchange(got_first, "rep", 1)
    got_first_other = core_swap(got_first)
    *so_far, rest = place([], shape, ema_proj, None, me, chip, core, [(0, weights, core_swap(weights))], 0)
    clip, _ = together(clip_factor, so_far[0])
    conv_results = adamw_step(param_conv, m_conv, v_conv, clip * conv_avg)
    got_second, *_ = together(got_second, *so_far, conv_results[0])
    got_second_other = core_swap(got_second)
    got_third, _ = together(got_third, got_second)
    first_block = jnp.where(odd, 1, 0)
    pieces = [
        (first_block, got_first, got_first_other),
        (1 - first_block, got_second, got_second_other),
        (2, got_third, core_swap(got_third)),
    ]
    full, new_ema = place(so_far, shape, None, rest, me, 1 - chip, core, pieces, 0)
    return (*results, new_ema, full, *conv_results)


def solution(mesh):
    in_specs = (
        P(("rep", "dp"), "tensor", None),
        P(("rep", "dp"), None, "tensor"),
        P("tensor", "dp"),
        P("tensor", "dp"),
        P("tensor", "dp"),
        P(("tensor", "dp"), None),
        P(None, "tensor"),
        P(None, "tensor"),
        P(None, "tensor"),
    )
    out_specs = (
        P("tensor", "dp"),
        P("tensor", "dp"),
        P("tensor", "dp"),
        P(("tensor", "dp"), None),
        P("tensor", None),
        P(None, "tensor"),
        P(None, "tensor"),
        P(None, "tensor"),
    )
    return jax.shard_map(body, mesh=mesh, in_specs=in_specs, out_specs=out_specs, check_vma=False)
```

```python
import math

import jax
import jax.numpy as jnp
from jax import lax
from jax.experimental import pallas as pl
from jax.experimental.pallas import tpu as pltpu
from jax.sharding import PartitionSpec as P

D = 1536
INNER = 3072
CONV = 3328
KCONV = 4

CORES = 2
CHUNKS = 3
LANES = 128
F16_SAFE_REPLICAS = 16
PARAMS = pltpu.CompilerParams(vmem_limit_bytes=16 * 2**20)
SMALL = pl.CostEstimate(flops=1, bytes_accessed=1024, transcendentals=1)


def adamw_step(param_in, first_in, second_in, grad_in):
    first_out = 0.9 * first_in + 0.1 * grad_in
    second_out = 0.95 * second_in + 0.05 * grad_in * grad_in
    bias_one = 1.0 - 0.9**10
    bias_two = 1.0 - 0.95**10
    update = first_out / bias_one / (jnp.sqrt(second_out / bias_two) + 1e-08)
    param_out = param_in - 0.25 * (update + 0.1 * param_in)
    return (param_out, first_out, second_out)


def clip_from(square_sum):
    clip_limit = 0.5 * math.sqrt(INNER * D + KCONV * CONV)
    return jnp.minimum(1.0, clip_limit / (jnp.sqrt(square_sum) + 1e-06))


def exchange(value, axis, step):
    return lax.ppermute(value, axis, [(i, i ^ step) for i in range(lax.axis_size(axis))])


def steps_of(axis, first=1):
    steps = []
    while first < lax.axis_size(axis):
        steps.append((axis, first))
        first *= 2
    return steps


def widen(x):
    return x.astype(jnp.float32)


def narrow(x):
    return x.astype(jnp.float16)


def together(*values):
    return lax.optimization_barrier(values)


def step_state(avgs, clip, param, first, second):
    rows, cols = param.shape
    chunks = len(avgs)
    part = rows // chunks

    def kernel(clip_ref, *refs):
        avg_refs, old_refs, new_refs = refs[:chunks], refs[chunks : chunks + 3], refs[chunks + 3 : chunks + 6]
        w_out, last_out, near, sems = refs[chunks + 6 :]
        loads, stores = [], []
        for k in range(chunks):
            at = pl.ds(k * part, part)
            for n in range(3):
                loads.append(pltpu.make_async_copy(old_refs[n].at[at, :], near.at[n, at, :], sems.at[3 * k + n]))
                loads[-1].start()
        for k in range(chunks):
            at = slice(k * part, (k + 1) * part)
            for load in loads[3 * k : 3 * k + 3]:
                load.wait()
            new = adamw_step(near[0, at], near[1, at], near[2, at], clip_ref[0, 0] * avg_refs[k][...])
            for n in range(3):
                near[n, at] = new[n]
                here = pl.ds(k * part, part)
                sem = sems.at[3 * (chunks + k) + n]
                stores.append(pltpu.make_async_copy(near.at[n, here, :], new_refs[n].at[here, :], sem))
                stores[-1].start()
            w_out[at, :] = new[0].astype(jnp.bfloat16)
            if k == chunks - 1:
                last_out[...] = new[0].astype(jnp.bfloat16)
        for store in stores:
            store.wait()

    far, close = pl.BlockSpec(memory_space=pltpu.HBM), pl.BlockSpec(memory_space=pltpu.VMEM)
    whole = jax.ShapeDtypeStruct((rows, cols), jnp.float32)
    return pl.pallas_call(
        kernel,
        in_specs=[pl.BlockSpec(memory_space=pltpu.SMEM)] + [close] * chunks + [far] * 3,
        out_specs=[far] * 3 + [close] * 2,
        out_shape=[whole, whole, whole]
        + [jax.ShapeDtypeStruct((rows, cols), jnp.bfloat16), jax.ShapeDtypeStruct((part, cols), jnp.bfloat16)],
        scratch_shapes=[pltpu.VMEM((3, rows, cols), jnp.float32), pltpu.SemaphoreType.DMA((6 * chunks,))],
        cost_estimate=SMALL,
        compiler_params=pltpu.CompilerParams(vmem_limit_bytes=50 * 2**20),
    )(clip, *avgs, param, first, second)


def place(so_far, shape, ema, rest, me, chip, core, pieces, written):
    rows, width = shape
    columns = width // 2
    cols = columns // CORES
    ema_rows = shape[0] // (width // cols)
    where = jnp.stack([jnp.int32(x) for x in (me, chip, core, *(block for block, _, _ in pieces))])
    values = [x for _, mine, theirs in pieces for x in (mine, theirs)]
    starts = rest is None

    def kernel(where_ref, old_ref, *refs):
        outs = 3 if starts else 2
        scratch = refs[-3:] if not starts else refs[-4:]
        full_out, ema_out = refs[-len(scratch) - outs : -len(scratch)][:2]
        near, new_near, sems = scratch[-3:]
        here = pl.ds(pl.multiple_of(where_ref[1] * columns, LANES), columns)
        if starts:
            rest_out, old_near = refs[-5], refs[-4]
            load = pltpu.make_async_copy(old_ref, old_near, sems.at[0])
            load.start()
        stores = []
        for k in range(len(pieces)):
            mine, theirs = refs[2 * k], refs[2 * k + 1]
            at = pl.ds(pl.multiple_of(where_ref[3 + k] * mine.shape[0], 16), mine.shape[0])

            @pl.when(where_ref[2] == 0)
            def _():
                near[at, :cols] = mine[...]
                near[at, cols:] = theirs[...]

            @pl.when(where_ref[2] != 0)
            def _():
                near[at, :cols] = theirs[...]
                near[at, cols:] = mine[...]

            if k >= written:
                stores.append(pltpu.make_async_copy(near.at[at, :], full_out.at[at, here], sems.at[2 + k]))
                stores[-1].start()
        mine_rows = near[pl.ds(pl.multiple_of(where_ref[0] * ema_rows, 16), ema_rows), :]
        if starts:
            load.wait()
            there = pl.ds(pl.multiple_of((1 - where_ref[1]) * columns, LANES), columns)
            new_near[...] = 0.9 * old_near[:, here] + 0.1 * widen(mine_rows)
            rest_out[...] = 0.9 * old_near[:, there]
        else:
            new_near[...] = old_ref[...] + 0.1 * widen(mine_rows)
        stores.append(pltpu.make_async_copy(new_near, ema_out.at[:, here], sems.at[1]))
        stores[-1].start()
        for store in stores:
            store.wait()

    far = pl.BlockSpec(memory_space=pltpu.HBM)
    close = pl.BlockSpec(memory_space=pltpu.VMEM)
    old = jax.ShapeDtypeStruct((ema_rows, width), jnp.float32)
    half = jax.ShapeDtypeStruct((ema_rows, columns), jnp.float32)
    return pl.pallas_call(
        kernel,
        in_specs=[pl.BlockSpec(memory_space=pltpu.SMEM), far if starts else close]
        + [close] * len(values)
        + [far] * len(so_far),
        out_specs=[far, far] + [close] * starts,
        out_shape=[jax.ShapeDtypeStruct(shape, jnp.bfloat16), old] + [half] * starts,
        input_output_aliases={2 + len(values) + i: i for i in range(len(so_far))},
        scratch_shapes=[pltpu.VMEM(old.shape, jnp.float32)] * starts
        + [
            pltpu.VMEM((rows, columns), jnp.bfloat16),
            pltpu.VMEM(half.shape, jnp.float32),
            pltpu.SemaphoreType.DMA((2 + len(pieces),)),
        ],
        cost_estimate=SMALL,
        compiler_params=pltpu.CompilerParams(vmem_limit_bytes=40 * 2**20),
    )(where, ema if starts else rest, *values, *so_far)


def body(grad_proj, grad_conv, param_proj, m_proj, v_proj, ema_proj, param_conv, m_conv, v_conv):
    reps, owners = lax.axis_size("rep"), lax.axis_size("dp")
    replica_count = reps * owners
    chips = owners // CORES
    rows, cols = param_proj.shape
    shape = (rows, cols * owners)
    me = lax.axis_index("dp")
    chip, core = me // CORES, me % CORES
    rep = lax.axis_index("rep")
    part_rows = rows // CHUNKS
    aligned = cols % LANES == 0 and part_rows % 16 == 0
    line = reps == 4

    def core_swap(x):
        return exchange(x, "dp", 1)

    def chip_shift(x, off):
        pairs = [
            (a * CORES + c, ((a + off) % chips) * CORES + c) for a in range(chips) for c in range(CORES)
        ]
        return lax.ppermute(x, "dp", pairs)

    def chunk(x, i):
        return x[i * part_rows : (i + 1) * part_rows]

    odd = rep % 2 == 1

    def either(values):
        return jnp.where(odd, values[1], values[0])

    scale = 1.0 / max(1, 2 ** math.ceil(math.log2(replica_count / F16_SAFE_REPLICAS)))
    inverse = 1.0 / (replica_count * scale)
    grad = grad_proj[0]

    def scaled(x):
        return x * scale if scale != 1.0 else x

    def block(owner_chip, owner_core, i):
        start = i * part_rows
        if owners != 4:
            owner = owner_chip * CORES + owner_core
            return scaled(lax.dynamic_slice(grad, (start, owner * cols), (part_rows, cols)))
        a, b, c, d = (grad[start : start + part_rows, n * cols : (n + 1) * cols] for n in range(owners))
        return scaled(jnp.where(owner_chip == 0, jnp.where(owner_core == 0, a, b), jnp.where(owner_core == 0, c, d)))

    targets = [(chip + off) % chips for off in (*range(1, chips), 0)]
    own = chips - 1
    gifts = {}

    def give(n, i, core):
        gifts[n, i] = core_swap(narrow(block(targets[n], 1 - core, i)))

    def chip_sum(n, i):
        return block(targets[n], core, i) + widen(gifts[n, i])

    for n in range(own):
        give(n, 0, core)
    outgoing = {(n, 0): narrow(chip_sum(n, 0)) for n in range(own)}
    later_core = core
    give(own, 0, later_core)
    for i in range(1, CHUNKS):
        for n in range(chips):
            give(n, i, later_core)

    avgs, squares = [None] * CHUNKS, [None] * CHUNKS
    sums, halves, totals = {}, {}, {}
    is_end = (rep == 0) | (rep == 3)
    conv_steps = [*steps_of("rep"), *steps_of("dp")]
    conv_sum = grad_conv[0]

    def average_of(total):
        return widen(total) * inverse

    def square_of(total):
        value = average_of(total)
        return jnp.sum(value * value, axis=0, keepdims=True)

    moving, own_sums = {}, {}

    def chip_sum_after(n, i, payloads):
        if i > 1:
            gifts[n, i] = together(gifts[n, i], *payloads)[0]
        total = chip_sum(n, i)
        return total if n == own else narrow(total)

    rounds = CHUNKS + 2 if line else CHUNKS
    for r in range(rounds + 1):
        names = list(moving)
        there = dict(zip(names, together(*[moving[k] for k in names]))) if names else {}
        moving, waiting = {}, {}
        for k, value in there.items():
            if k[0] == "own":
                own_sums[k[1]] = value
            elif k[0] == "average":
                avgs[k[1]] = value
            elif k[0] == "square":
                squares[k[1]] = value
            elif k[0] == "outgoing":
                outgoing[k[1:]] = value

        if 0 <= r - 1 < CHUNKS:
            total = own_sums[r - 1]
            for n in range(own):
                total = total + widen(there["chips", n])
            sums[r - 1] = narrow(total) if line else lax.psum(total, "rep")
        if ("pair", 0) in there:
            i = r - 2
            if i < CHUNKS:
                halves[i] = narrow(widen(sums[i]) + widen(there["pair", 0]))
            if i >= 2:
                waiting["average", i - 2] = average_of(jnp.where(is_end, there["pair", 0], totals[i - 2]))
        if ("middle", 0) in there:
            totals[r - 3] = narrow(widen(halves[r - 3]) + widen(there["middle", 0]))
            if r < rounds:
                waiting["square", r - 3] = square_of(totals[r - 3])
            else:
                squares[r - 3] = square_of(together(totals[r - 3])[0])
        if ("conv", 0) in there:
            conv_sum = there["own conv", 0] + there["conv", 0]

        payloads = []
        if line and 0 <= r - 2 < CHUNKS:
            payloads.append(halves[r - 2])
            moving["middle", 0] = lax.ppermute(halves[r - 2], "rep", [(1, 2), (2, 1)])
        if r < CHUNKS:
            for n in range(own):
                payloads.append(outgoing[n, r])
                moving["chips", n] = chip_shift(payloads[-1], n + 1)
        i = r - 1
        if line and 0 <= i < CHUNKS + 2:
            if i < 2:
                payload = sums[i]
            elif i < CHUNKS:
                payload = jnp.where(is_end, sums[i], totals[i - 2])
            else:
                payload = totals[i - 2]
            payloads.append(payload)
            moving["pair", 0] = lax.ppermute(payload, "rep", [(0, 1), (1, 0), (2, 3), (3, 2)])
        if r < CHUNKS:
            if r + 1 < CHUNKS:
                for n in range(own):
                    waiting["outgoing", n, r + 1] = chip_sum_after(n, r + 1, payloads)
            waiting["own", r] = chip_sum_after(own, r, payloads)
        if conv_steps and payloads:
            sent, *_ = together(conv_sum, *payloads, *(waiting[k] for k in waiting if k[0] == "outgoing"))
            moving["own conv", 0] = sent
            moving["conv", 0] = exchange(sent, *conv_steps.pop(0))
        moving.update(waiting)

    if not line:
        avgs = [average_of(sums[i]) for i in range(CHUNKS)]
        squares = [square_of(sums[i]) for i in range(CHUNKS)]
    for step in conv_steps:
        conv_sum = conv_sum + exchange(conv_sum, *step)
    conv_avg = conv_sum / replica_count
    conv_square = jnp.sum(conv_avg * conv_avg)

    square = sum(squares[1:], squares[0])
    square = square + jnp.where(me == 0, conv_square, 0.0) * (lax.broadcasted_iota(jnp.int32, square.shape, 1) == 0)
    if square.shape[1] % LANES == 0:
        square = jnp.sum(square.reshape(-1, LANES), axis=0, keepdims=True)
    hops = [*steps_of("dp"), *steps_of("tensor")]
    for step in hops if not line else hops[:-1]:
        square = square + exchange(square, *step)
    if line:
        size, step = lax.axis_size("tensor"), hops[-1][1]
        across = [(a * size + t, (a ^ 1) * size + (t ^ step)) for a in range(reps) for t in range(size)]
        theirs = lax.ppermute(square, ("rep", "tensor"), across)
        inner, other = exchange(square, "rep", 1), exchange(square, *hops[-1])
        square = jnp.where(is_end, inner, square) + jnp.where(is_end, theirs, other)
        arrived = moving["pair", 0]
        for n in range(CHUNKS - 1):
            if avgs[n] is None:
                avgs[n] = moving["average", n]
    clip_factor = clip_from(jnp.sum(square, keepdims=True))

    def last_average(after):
        if not line:
            return avgs[-1]
        return average_of(jnp.where(is_end, together(arrived, after)[0], totals[CHUNKS - 1]))

    if not (aligned and chips == 2 and reps % 2 == 0 and CHUNKS == 3):
        avgs[-1] = last_average(clip_factor)
        results = adamw_step(param_proj, m_proj, v_proj, clip_factor * jnp.concatenate(avgs))
        weights = results[0].astype(jnp.bfloat16)
        full = jnp.zeros(shape, jnp.bfloat16)
        for piece, owner in ((weights, me), (core_swap(weights), me ^ 1)):
            full = lax.dynamic_update_slice(full, piece, (0, owner * cols))
        for off in range(1, chips):
            got = chip_shift(weights, off)
            from_chip = (chip - off) % chips
            for piece, owner in ((got, from_chip * CORES + core), (core_swap(got), from_chip * CORES + 1 - core)):
                full = lax.dynamic_update_slice(full, piece, (0, owner * cols))
        conv_results = adamw_step(param_conv, m_conv, v_conv, clip_factor * conv_avg)
        ema_count = ema_proj.shape[0]
        row_block = lax.dynamic_slice_in_dim(full, me * ema_count, ema_count, 0)
        return (*results, 0.9 * ema_proj + 0.1 * widen(row_block), full, *conv_results)

    g = either(avgs)
    start = jnp.where(odd, part_rows, 0)
    p, m, v = (lax.dynamic_slice(x, (start, 0), (part_rows, cols)) for x in (param_proj, m_proj, v_proj))
    first = adamw_step(p, m, v, clip_factor * g)[0].astype(jnp.bfloat16)
    got_first = chip_shift(first, 1)
    avgs[-1] = last_average(first)
    *results, weights, third = step_state(avgs, clip_factor, param_proj, m_proj, v_proj)
    weights, got_first = together(weights, got_first)

    got_third = chip_shift(third, 1)
    got_second = exchange(got_first, "rep", 1)
    got_first_other = core_swap(got_first)
    *so_far, rest = place([], shape, ema_proj, None, me, chip, core, [(0, weights, core_swap(weights))], 0)
    clip, _ = together(clip_factor, so_far[0])
    conv_results = adamw_step(param_conv, m_conv, v_conv, clip * conv_avg)
    got_second, *_ = together(got_second, *so_far, conv_results[0])
    got_second_other = core_swap(got_second)
    got_third, _ = together(got_third, got_second)
    first_block = jnp.where(odd, 1, 0)
    pieces = [
        (first_block, got_first, got_first_other),
        (1 - first_block, got_second, got_second_other),
        (2, got_third, core_swap(got_third)),
    ]
    full, new_ema = place(so_far, shape, None, rest, me, 1 - chip, core, pieces, 0)
    return (*results, new_ema, full, *conv_results)


def solution(mesh):
    in_specs = (
        P(("rep", "dp"), "tensor", None),
        P(("rep", "dp"), None, "tensor"),
        P("tensor", "dp"),
        P("tensor", "dp"),
        P("tensor", "dp"),
        P(("tensor", "dp"), None),
        P(None, "tensor"),
        P(None, "tensor"),
        P(None, "tensor"),
    )
    out_specs = (
        P("tensor", "dp"),
        P("tensor", "dp"),
        P("tensor", "dp"),
        P(("tensor", "dp"), None),
        P("tensor", None),
        P(None, "tensor"),
        P(None, "tensor"),
        P(None, "tensor"),
    )
    return jax.shard_map(body, mesh=mesh, in_specs=in_specs, out_specs=out_specs, check_vma=False)
```
